256 devices in a mesh: section: 4 (over y), node: 64 (over z, x, core).
Axes of the slice: x: 4, y: 4, z: 8, core: 2. Of those that a mesh axis runs over, the one named last changes fastest.
Arguments:
- master: float32 [4, 1024, 3072], P('section', 'node'), may hold values from -0.1875 to 0.1875
- first_moment: float32 [4, 1024, 3072], P('section', 'node'), may hold values from -6 to 6
- second_moment: float32 [4, 1024, 3072], P('section', 'node'), may hold values from 1 to 100
- node_state: bfloat16 [2, 4096, 1024], P(None, 'node'), may hold values from -6 to 6
- obs_rows: bfloat16 [2, 8192, 247], P(None, 'node'), may hold values from -6 to 6
- obs_device: int32 [2, 8192, 1], P(None, 'node'), may hold values from 0 to 63; in each aligned block of 128 rows (0 to 127, 128 to 255, ..., all dimensions but the last counted through in order) at most 4 rows name the same one
- obs_node: int32 [2, 8192], P(None, 'node'), may hold values from 0 to 63
- encode_weight: bfloat16 [247, 1024], replicated, may hold values from -0.375 to 0.375
- decode_weight: bfloat16 [1024, 247], replicated, may hold values from -0.1875 to 0.1875
- neighbors: int32 [4096, 16], P('node'), may hold values from 0 to 4095, as said below
- neighbor_count: int32 [4096], P('node'), may hold values from 1 to 16, as said below
- out_grad: bfloat16 [2, 4096, 247], P(None, 'node'), may hold values from -6 to 6
Outputs:
- new_weights: float32 [4, 1024, 3072], P('section', 'node')
- new_first: float32 [4, 1024, 3072], P('section', 'node')
- new_second: float32 [4, 1024, 3072], P('section', 'node')
The draws below stay inside these ranges and needn't reach their ends.
Inputs may be any that keep to these rules, and one draw needn't show every extreme that they name: `obs_device`: in each micro-batch, the 128 profiles held by one index of node name one owner index at most 4 times. `neighbors`: the 16 ids of a node are distinct and each lies within 32 of the node's own id, counted cyclically over 4096 nodes. `neighbor_count`: slots at or past a node's count are padding.
All inputs are finite; a program needn't handle non-finite values.
Results may differ from the reference program's by a relative error of at most 0.015.
Values may be sent and summed in bfloat16 or wider, within the bound.
No kernel may reach another device: no remote copies, remote signals or barrier semaphores. Data moves between devices by JAX's collectives and lax.ppermute only.
A program may use at most 192 MiB of HBM per device.

```python
import math
import jax
import jax.numpy as jnp
import numpy as np
from jax import lax

D = 1024
HEADS = 8
LEVELS = 247
NBR_SLOTS = 16
HALO_W = 32
MICRO = 2
STEP = 100
NODES_DEV = 64
OBS_DEV = 128
HEAD_DIM = 128
SECTIONS = 4
NODES = 4096
OBS = 8192
CAP = 4
N_NODE = 64


def draw_neighbors(key, part):
    window = 2 * HALO_W + 1
    random_keys = jax.random.randint(key, (NODES, window), 0, 1 << 20)
    scored = random_keys * window + jnp.arange(window)[None, :]
    chosen = jnp.argsort(scored, axis=1)[:, :NBR_SLOTS]
    node_ids = (jnp.arange(NODES)[:, None] + chosen - HALO_W) % NODES
    return node_ids.astype(jnp.int32)


def draw_neighbor_count(key, part):
    counts = jax.random.randint(key, (NODES,), 1, NBR_SLOTS + 1)
    return counts.at[0].set(NBR_SLOTS).at[1].set(1).astype(jnp.int32)


def place_ends(entries, own_key, low, high):
    longest = entries.shape.index(max(entries.shape))
    spots = []
    for shift in (0, 1):
        where = [jax.random.randint(jax.random.fold_in(own_key, axis), (), 0, length) for axis, length in enumerate(entries.shape)]
        where[longest] = (where[longest] + shift) % entries.shape[longest]
        spots.append(tuple(where))
    return entries.at[spots[0]].set(low).at[spots[1]].set(high)


def block_scale(key, shape, split, smallest, high):
    def one(axis_at, blocks):
        draws = jax.random.uniform(jax.random.fold_in(jax.random.fold_in(key, 6), axis_at), (blocks,), jnp.float32, smallest / len(split), high / len(split))
        return jnp.repeat(jnp.exp(draws), shape[axis_at] // blocks).reshape((-1,) + (1,) * (len(shape) - axis_at - 1))

    level = one(*split[0])
    for cut in split[1:]:
        level = level * one(*cut)
    return level


def shared_out(rng, own, number, rows, count, top, limit, lean):
    order = jax.random.permutation(rng, count)
    heavy_load, usual = load_shares(count, rows * top, limit, lean, True), load_shares(count, rows * top, limit, lean, False)
    places = jnp.arange(count)

    def named(tallies, rotation):
        used = int((tallies > 0).sum())
        fixed = max(1, used // 4)
        moved = fixed + (places - fixed + rotation * (used - fixed)) % max(1, count - fixed)
        return jnp.zeros((count,), jnp.int32).at[order[jnp.where(places < fixed, places, moved)]].set(jnp.asarray(tallies, jnp.int32))

    tallies = jnp.where(number % 4 == 0, named(heavy_load, number // 4), named(usual, number - number // 4 - 1))
    mixed = jax.random.permutation(jax.random.fold_in(own, 3), count)
    source_of, sink = mixed[0:count // 2 * 2:2], mixed[1:count // 2 * 2:2]
    room = jnp.minimum(tallies[source_of] - 1, limit - tallies[sink]) // 2
    room = jnp.where((source_of == order[0]) | (sink == order[0]) | (tallies[sink] == 0), 0, jnp.maximum(room, 0))
    moved = jax.random.randint(jax.random.fold_in(own, 4), (count // 2,), 0, 1 << 20) % (room + 1)
    tallies = tallies.at[source_of].add(-moved).at[sink].add(moved)
    labels = jnp.searchsorted(jnp.cumsum(tallies), jnp.arange(rows * top), side="right").astype(jnp.int32)
    grid = labels.reshape(top, rows).T
    grid = grid[jax.random.permutation(jax.random.fold_in(own, 1), rows)]
    rotation = jax.random.randint(jax.random.fold_in(own, 2), (rows, 1), 0, top)
    return jnp.take_along_axis(grid, (jnp.arange(top)[None, :] + rotation) % top, axis=1)


def load_shares(number_of, total, most, slope, full):
    portions = [(1 << 20) // math.isqrt(grade ** slope) + 1 for grade in range(1, number_of + 1)]
    largest = most if full else min(most, max(-(-total // number_of), total * portions[0] // sum(portions)))
    least = 1 if total - largest >= number_of - 1 else 0
    holding, spare = [largest] + [least] * (number_of - 1), total - largest - least * (number_of - 1)
    while spare > 0:
        candidates = [i for i in range(1, number_of) if holding[i] < largest] or [i for i in range(1, number_of) if holding[i] < most]
        mass, remaining = sum([portions[i] for i in candidates]), spare
        for i in candidates:
            addition = min(most - holding[i], max(1, remaining * portions[i] // mass), spare)
            holding[i] = holding[i] + addition
            spare = spare - addition
    return np.array(holding)


def noise(stream_key, shape, deviation, most, split=(), held_as=jnp.bfloat16):
    entries = jax.random.normal(stream_key, shape, jnp.float32) * deviation
    if len(split) > 0:
        entries = block_scale(stream_key, shape, split, -0.22, 0.18) * entries
    return jnp.clip(entries, min=-most, max=most).astype(held_as)


def setup_inputs(seed: int = 0) -> dict:
    key_list = jax.random.split(jax.random.key(seed), 13)
    master = noise(key_list[0], (SECTIONS, D, 3 * D), D ** -0.5, 0.1875, ((0, 4), (1, 64)), jnp.float32)
    first_moment = noise(key_list[1], (SECTIONS, D, 3 * D), 1.0, 6.0, ((0, 4), (1, 64)), jnp.float32)
    second_moment = jnp.clip(jnp.exp(math.log(100.0) - 4.6051702 * jax.random.uniform(key_list[2], (SECTIONS, D, 3 * D), jnp.float32) ** block_scale(key_list[2], (SECTIONS, D, 3 * D), ((0, 4), (1, 64)), -0.2, 0.2)), 1.0, 100.0)
    node_state = noise(key_list[3], (MICRO, NODES, D), 1.0, 6.0, ((1, 64),))
    obs_rows = noise(key_list[4], (MICRO, OBS, LEVELS), 1.0, 6.0, ((1, 64),))
    obs_device_keys = jax.random.split(jax.random.fold_in(key_list[5], 1), MICRO * OBS // OBS_DEV)
    obs_device_turns = jax.random.permutation(jax.random.fold_in(key_list[5], 3), MICRO * OBS // OBS_DEV)
    obs_device = jax.vmap(lambda own, number: shared_out(jax.random.fold_in(key_list[5], 2), own, number, OBS_DEV, N_NODE, 1, CAP, 2))(obs_device_keys, obs_device_turns).reshape((MICRO, OBS, 1))
    obs_node = place_ends(jax.random.randint(key_list[6], (MICRO, OBS), 0, NODES_DEV), jax.random.fold_in(key_list[6], 1), 0, NODES_DEV - 1).astype(jnp.int32)
    encode_weight = noise(key_list[7], (LEVELS, D), LEVELS ** -0.5, 0.375)
    decode_weight = noise(key_list[8], (D, LEVELS), D ** -0.5, 0.1875)
    neighbors = draw_neighbors(jax.random.fold_in(key_list[12], 71), 0)
    neighbor_count = draw_neighbor_count(jax.random.fold_in(key_list[12], 71), 0)
    out_grad = noise(key_list[11], (MICRO, NODES, LEVELS), 1.0, 6.0, ((1, 64),))
    return {"master": master, "first_moment": first_moment, "second_moment": second_moment, "node_state": node_state, "obs_rows": obs_rows, "obs_device": obs_device, "obs_node": obs_node, "encode_weight": encode_weight, "decode_weight": decode_weight, "neighbors": neighbors, "neighbor_count": neighbor_count, "out_grad": out_grad}


BETA_ONE = 0.9
BETA_TWO = 0.999
LEARN_RATE = 0.001

def norm_rows(values):
    return values * lax.rsqrt(lax.optimization_barrier(jnp.mean(values * values, axis=-1, keepdims=True)) + 1e-06)

def attend_rows(state, query, keys, values_rows, valid):
    count = query.shape[0]
    query = query.reshape(count, HEADS, HEAD_DIM)
    keys = keys.reshape(count, NBR_SLOTS, HEADS, HEAD_DIM)
    values_rows = values_rows.reshape(count, NBR_SLOTS, HEADS, HEAD_DIM)
    scores = jnp.einsum('nhc,njhc->nhj', query, keys, precision=lax.Precision.HIGHEST) * HEAD_DIM ** (-0.5)
    weight = jnp.exp(scores) * valid[:, None, :]
    probs = weight / lax.optimization_barrier(jnp.sum(weight, axis=-1, keepdims=True))
    rounded = lax.optimization_barrier(probs.astype(jnp.bfloat16)).astype(jnp.float32)
    mixed = jnp.einsum('nhj,njhc->nhc', rounded, values_rows, precision=lax.Precision.HIGHEST)
    return state + mixed.reshape(count, D)

def attend_all(state, query, key_value, neighbors, valid):

    def one_block(pieces):
        rows_state, rows_query, rows_nbr, rows_valid = pieces
        gathered = key_value[rows_nbr]
        return attend_rows(rows_state, rows_query, gathered[..., :D], gathered[..., D:], rows_valid)
    blocks = lax.map(one_block, (state.reshape(N_NODE, NODES_DEV, D), query.reshape(N_NODE, NODES_DEV, D), neighbors.reshape(N_NODE, NODES_DEV, NBR_SLOTS), valid.reshape(N_NODE, NODES_DEV, NBR_SLOTS)))
    return blocks.reshape(NODES, D)

def reference(master, first_moment, second_moment, node_state, obs_rows, obs_device, obs_node, encode_weight, decode_weight, neighbors, neighbor_count, out_grad):
    valid = (jnp.arange(NBR_SLOTS)[None, :] < neighbor_count[:, None]).astype(jnp.float32)
    owner = obs_device[..., 0] * NODES_DEV + obs_node + jnp.arange(MICRO).astype(jnp.int32)[:, None] * NODES
    embedded = jnp.dot(obs_rows.reshape(-1, LEVELS), encode_weight, preferred_element_type=jnp.float32)
    encoded = jax.ops.segment_sum(embedded, owner.reshape(-1), num_segments=MICRO * NODES).reshape(MICRO, NODES, D)
    entry = (node_state.astype(jnp.float32) + encoded).astype(jnp.bfloat16)
    weights = master.astype(jnp.bfloat16)
    grads = jnp.zeros(master.shape, jnp.float32)
    for batch in range(MICRO):
        current = entry[batch]
        saved = []
        for section in range(SECTIONS):
            state = current.astype(jnp.float32)
            normed = norm_rows(state).astype(jnp.bfloat16)
            projected = jnp.dot(normed, weights[section], preferred_element_type=jnp.float32).astype(jnp.bfloat16)
            query = projected[:, :D].astype(jnp.float32)
            key_value = projected[:, D:].astype(jnp.float32)
            saved.append((state, normed, query, key_value))
            current = attend_all(state, query, key_value, neighbors, valid).astype(jnp.bfloat16)
        upstream = lax.dot_general(out_grad[batch], decode_weight, (((1,), (1,)), ((), ())), preferred_element_type=jnp.float32).astype(jnp.bfloat16)
        for section in reversed(range(SECTIONS)):
            state, normed, query, key_value = saved[section]
            _, pull = jax.vjp(lambda a, b, c: attend_all(a, b, c, neighbors, valid), state, query, key_value)
            grad_state, grad_query, grad_kv = pull(upstream.astype(jnp.float32))
            grad_qkv = jnp.concatenate([grad_query, grad_kv], axis=1).astype(jnp.bfloat16)
            grads = grads.at[section].add(lax.dot_general(normed, grad_qkv, (((0,), (0,)), ((), ())), preferred_element_type=jnp.float32))
            grad_normed = lax.dot_general(grad_qkv, weights[section], (((1,), (1,)), ((), ())), preferred_element_type=jnp.float32)
            _, pull_norm = jax.vjp(norm_rows, state)
            grad_norm, = pull_norm(grad_normed)
            upstream = (grad_state + grad_norm).astype(jnp.bfloat16)
    new_first = BETA_ONE * first_moment + (1.0 - BETA_ONE) * grads
    new_second = BETA_TWO * second_moment + (1.0 - BETA_TWO) * grads * grads
    step_size = new_first / (1.0 - BETA_ONE ** STEP) / (jnp.sqrt(new_second / (1.0 - BETA_TWO ** STEP)) + 1e-08)
    new_weights = master - LEARN_RATE * step_size
    return (new_weights, new_first, new_second)
```

```python
import jax
import jax.numpy as jnp
from jax import lax
from jax.experimental import pallas as pl
from jax.experimental.pallas import tpu as pltpu
from jax.sharding import Mesh, PartitionSpec as P

HEADS = 8
HALO_W = 32
STEP = 100


BETA_ONE = 0.9
BETA_TWO = 0.999
LEARN_RATE = 0.001

NODE = ("z", "x", "core")
PLANE = ("x", "core")
F32 = jnp.float32
BF16 = jnp.bfloat16


def ring(steps):
    count = lax.axis_size(NODE)
    return [(i, (i + steps) % count) for i in range(count)]


def from_behind(value, axis, steps):
    count = lax.axis_size(axis)
    leading, last = (max(0, -steps), min(count, count - steps))
    return lax.ppermute(value, axis, [(source, source + steps) for source in range(leading, last)])


def norm_rows(values):
    return values * lax.rsqrt(jnp.mean(values * values, axis=-1, keepdims=True) + 1e-06)


def norm_pull(values, grads):
    scale = lax.rsqrt(jnp.mean(values * values, axis=-1, keepdims=True) + 1e-06)
    inner = jnp.mean(values * grads, axis=-1, keepdims=True)
    return scale * (grads - values * (inner * scale * scale))


def band(low_ref, proj_ref, high_ref, start, offset, size):
    return jnp.concatenate(
        [
            low_ref[:, start : start + size],
            proj_ref[:, offset + start : offset + start + size],
            high_ref[:, start : start + size],
        ],
        axis=0,
    )


def nt(a, b):
    return lax.dot_general(a, b, (((1,), (1,)), ((), ())), preferred_element_type=F32)


def nn(a, b):
    return lax.dot_general(a, b, (((1,), (0,)), ((), ())), preferred_element_type=F32)


def tn(a, b):
    return lax.dot_general(a, b, (((0,), (0,)), ((), ())), preferred_element_type=F32)


def attend_kernel(state_ref, proj_ref, low_ref, high_ref, mask_ref, out_ref):
    width = state_ref.shape[1]
    size = width // HEADS
    used = mask_ref[...] > 0
    for head in range(HEADS):
        a, b = head * size, (head + 1) * size
        keys = band(low_ref, proj_ref, high_ref, a, width, size)
        values = band(low_ref, proj_ref, high_ref, width + a, width, size)
        scores = nt(proj_ref[:, a:b], keys) * size ** (-0.5)
        weight = jnp.where(used, jnp.exp(scores), 0.0)
        probs = weight / jnp.sum(weight, axis=-1, keepdims=True)
        mixed = nn(probs.astype(BF16), values)
        out_ref[:, a:b] = (state_ref[:, a:b].astype(F32) + mixed).astype(BF16)


def attend(state, proj, low, high, mask):
    return pl.pallas_call(
        attend_kernel,
        out_shape=jax.ShapeDtypeStruct(state.shape, BF16),
        in_specs=[pl.BlockSpec(memory_space=pltpu.VMEM)] * 5,
        out_specs=pl.BlockSpec(memory_space=pltpu.VMEM),
        name="attend",
    )(state, proj, low, high, mask)


def pull_kernel(proj_ref, low_ref, high_ref, mask_ref, up_ref, query_ref, own_ref, low_out, high_out):
    width = up_ref.shape[1]
    size = width // HEADS
    rim = low_ref.shape[0]
    rows = proj_ref.shape[0]
    used = mask_ref[...] > 0
    for head in range(HEADS):
        a, b = head * size, (head + 1) * size
        query = proj_ref[:, a:b]
        keys = band(low_ref, proj_ref, high_ref, a, width, size)
        values = band(low_ref, proj_ref, high_ref, width + a, width, size)
        upstream = up_ref[:, a:b]
        scores = nt(query, keys) * size ** (-0.5)
        weight = jnp.where(used, jnp.exp(scores), 0.0)
        probs = weight / jnp.sum(weight, axis=-1, keepdims=True)
        grad_probs = nt(upstream, values).astype(BF16).astype(F32)
        inner = jnp.sum(grad_probs * probs, axis=-1, keepdims=True)
        grad_scores = (probs * (grad_probs - inner) * size ** (-0.5)).astype(BF16)
        query_ref[:, a:b] = nn(grad_scores, keys).astype(BF16)
        for base, grad in ((0, tn(grad_scores, query)), (width, tn(probs.astype(BF16), upstream))):
            c, d = base + a, base + b
            low_out[:, c:d] = grad[:rim].astype(BF16)
            own_ref[:, c:d] = grad[rim : rim + rows]
            high_out[:, c:d] = grad[rim + rows :].astype(BF16)


def attend_pull(proj, low, high, mask, upstream):
    rows, width = upstream.shape
    rim = low.shape[0]
    return pl.pallas_call(
        pull_kernel,
        out_shape=(
            jax.ShapeDtypeStruct((rows, width), BF16),
            jax.ShapeDtypeStruct((rows, 2 * width), F32),
            jax.ShapeDtypeStruct((rim, 2 * width), BF16),
            jax.ShapeDtypeStruct((rim, 2 * width), BF16),
        ),
        in_specs=[pl.BlockSpec(memory_space=pltpu.VMEM)] * 5,
        out_specs=[pl.BlockSpec(memory_space=pltpu.VMEM)] * 4,
        name="attend_pull",
    )(proj, low, high, mask, upstream)


def route(obs_rows, obs_device, obs_node, encode_weight, node_state):
    micro, nodes_dev, width = node_state.shape
    per_dev, levels = obs_rows.shape[1:]
    node_devs = lax.axis_size(NODE)
    capacity = max(2, 2 * per_dev // node_devs)
    slots = node_devs * micro * capacity
    target = obs_device[..., 0]
    named = (target[..., None] == jnp.arange(node_devs)[None, None, :]).astype(BF16)
    earlier = (jnp.arange(per_dev)[:, None] > jnp.arange(per_dev)[None, :]).astype(BF16)
    before = jnp.einsum("ij,mjd->mid", earlier, named, preferred_element_type=F32)
    ranked = jnp.sum(before * named.astype(F32), axis=-1).astype(jnp.int32)
    position = (target * micro + jnp.arange(micro)[:, None]) * capacity + ranked
    chosen = (jnp.arange(slots)[:, None] == position.reshape(1, -1)).astype(BF16)
    payload = jnp.concatenate([obs_rows, obs_node[..., None].astype(BF16)], axis=-1)
    sent = nn(chosen, payload.reshape(micro * per_dev, levels + 1)).astype(BF16)
    received = lax.all_to_all(
        sent.reshape(node_devs, micro * capacity, levels + 1),
        NODE,
        split_axis=0,
        concat_axis=0,
        tiled=True,
    ).reshape(slots, levels + 1)
    owner = received[:, levels].astype(jnp.int32)
    owner = owner + (jnp.arange(slots) // capacity % micro) * nodes_dev
    held = (jnp.arange(micro * nodes_dev)[:, None] == owner[None, :]).astype(BF16)
    summed = nn(held, received[:, :levels])
    high = lax.reduce_precision(summed, 8, 7)
    rest = summed - high
    encoded = nn(high.astype(BF16), encode_weight) + nn(rest.astype(BF16), encode_weight)
    return (node_state.astype(F32) + encoded.reshape(micro, nodes_dev, width)).astype(BF16)


def body(
    master,
    first_moment,
    second_moment,
    node_state,
    obs_rows,
    obs_device,
    obs_node,
    encode_weight,
    decode_weight,
    neighbors,
    neighbor_count,
    out_grad,
):
    sections = lax.axis_size("section")
    section = lax.axis_index("section")
    node_devs = lax.axis_size(NODE)
    micro, nodes_dev, width = node_state.shape
    total_nodes = nodes_dev * node_devs
    anchor = lax.axis_index(NODE) * nodes_dev
    weight_full = lax.all_gather(master[0].astype(BF16), NODE, axis=0, tiled=True)
    entry = route(obs_rows, obs_device, obs_node, encode_weight, node_state)
    rim = HALO_W
    relative = (neighbors - anchor) % total_nodes
    relative = jnp.where(relative >= total_nodes - rim, relative - total_nodes, relative) + rim
    extent = nodes_dev + 2 * rim
    valid = jnp.arange(neighbors.shape[1])[None, :] < neighbor_count[:, None]
    at = (relative[..., None] == jnp.arange(extent)[None, None, :]) & valid[..., None]
    mask = jnp.sum(at.astype(F32), axis=1)

    ticks = micro + sections - 1
    incoming = jnp.zeros((nodes_dev, width), BF16)
    saved = []
    kept_normed = [jnp.zeros((nodes_dev, width), BF16)] * micro
    for tick in range(ticks):
        state = jnp.where(section == 0, entry[min(tick, micro - 1)], incoming)
        normed = norm_rows(state.astype(F32)).astype(BF16)
        proj = nn(normed, weight_full).astype(BF16)
        low = lax.ppermute(proj[nodes_dev - rim :, width:], NODE, ring(1))
        high = lax.ppermute(proj[:rim, width:], NODE, ring(-1))
        saved.append((state, proj, low, high))
        for batch in range(micro):
            kept_normed[batch] = jnp.where(section == tick - batch, normed, kept_normed[batch])
        if tick + 1 < ticks:
            incoming = from_behind(attend(state, proj, low, high, mask), "section", 1)
    normed_all = lax.all_gather(jnp.stack(kept_normed), PLANE, axis=0, tiled=False)

    head_grad = nt(out_grad.reshape(micro * nodes_dev, -1), decode_weight)
    head_grad = head_grad.astype(BF16).reshape(micro, nodes_dev, width)
    returning = jnp.zeros((nodes_dev, width), BF16)
    plane = lax.axis_size(PLANE)
    columns = 3 * width // plane
    kept_grad = [jnp.zeros((nodes_dev, 3 * width), BF16)] * micro
    gathered = []
    for tick in range(ticks):
        sources = {}
        for stage in range(sections):
            batch = tick - (sections - 1) + stage
            if 0 <= batch < micro:
                sources[stage] = (batch, batch + stage)
        stages = sorted(sources)
        state, proj, low, high = saved[sources[stages[0]][1]]
        for stage in stages[1:]:
            here = section == stage
            state, proj, low, high = (
                jnp.where(here, a, b)
                for a, b in zip(saved[sources[stage][1]], (state, proj, low, high))
            )
        upstream = returning
        if sections - 1 in sources:
            upstream = jnp.where(
                section == sections - 1, head_grad[sources[sections - 1][0]], returning
            )
        grad_query, own, low_edge, high_edge = attend_pull(proj, low, high, mask, upstream)
        from_low = lax.ppermute(high_edge, NODE, ring(1))
        from_high = lax.ppermute(low_edge, NODE, ring(-1))
        own = own + jnp.concatenate([from_low, from_high], axis=0).astype(F32)
        grad_qkv = jnp.concatenate([grad_query, own.astype(BF16)], axis=1)
        for stage in stages:
            batch = sources[stage][0]
            kept_grad[batch] = jnp.where(section == stage, grad_qkv, kept_grad[batch])
        if tick + 1 < ticks:
            grad_normed = nt(grad_qkv, weight_full)
            downward = (upstream.astype(F32) + norm_pull(state.astype(F32), grad_normed)).astype(
                BF16
            )
            returning = from_behind(downward, "section", -1)
        batch = tick - (sections - 1)
        if batch >= 0:
            parts = kept_grad[batch].reshape(nodes_dev, plane, columns).transpose(1, 0, 2)
            gathered.append(
                lax.all_to_all(parts, PLANE, split_axis=0, concat_axis=0, tiled=True)
            )
    partial = sum(
        tn(
            normed_all[:, batch].reshape(plane * nodes_dev, width),
            gathered[batch].reshape(plane * nodes_dev, columns),
        )
        for batch in range(micro)
    )
    rows = width // node_devs
    pieces = lax.all_to_all(
        partial.astype(BF16).reshape(node_devs, rows, columns),
        NODE,
        split_axis=0,
        concat_axis=0,
        tiled=True,
    )
    pieces = pieces.reshape(node_devs // plane, plane, rows, columns).astype(F32)
    gradient = jnp.sum(pieces, axis=0).transpose(1, 0, 2).reshape(1, rows, 3 * width)
    new_first = BETA_ONE * first_moment + (1.0 - BETA_ONE) * gradient
    new_second = BETA_TWO * second_moment + (1.0 - BETA_TWO) * gradient * gradient
    step_size = (
        new_first / (1.0 - BETA_ONE**STEP) / (jnp.sqrt(new_second / (1.0 - BETA_TWO**STEP)) + 1e-08)
    )
    new_weights = master - LEARN_RATE * step_size
    return (new_weights, new_first, new_second)


def solution(mesh):
    sections, node_devs = mesh.devices.shape
    fine = Mesh(mesh.devices.reshape(sections, node_devs // 8, 4, 2), ("section",) + NODE)
    in_specs = (
        P("section", NODE, None),
        P("section", NODE, None),
        P("section", NODE, None),
        P(None, NODE, None),
        P(None, NODE, None),
        P(None, NODE, None),
        P(None, NODE),
        P(),
        P(),
        P(NODE, None),
        P(NODE),
        P(None, NODE, None),
    )
    out_specs = (P("section", NODE, None), P("section", NODE, None), P("section", NODE, None))
    return jax.shard_map(body, mesh=fine, in_specs=in_specs, out_specs=out_specs, check_vma=False)
```

```python
import jax
import jax.numpy as jnp
from jax import lax
from jax.experimental import pallas as pl
from jax.experimental.pallas import tpu as pltpu
from jax.sharding import Mesh, PartitionSpec as P

HEADS = 8
HALO_W = 32
STEP = 100


BETA_ONE = 0.9
BETA_TWO = 0.999
LEARN_RATE = 0.001

NODE = ("z", "x", "core")
PLANE = ("x", "core")
F32 = jnp.float32
BF16 = jnp.bfloat16
KERNEL_VMEM = 8 * 2**20


def ring(steps):
    count = lax.axis_size(NODE)
    return [(i, (i + steps) % count) for i in range(count)]


def from_behind(value, axis, steps):
    count = lax.axis_size(axis)
    leading, last = (max(0, -steps), min(count, count - steps))
    return lax.ppermute(value, axis, [(source, source + steps) for source in range(leading, last)])


def norm_rows(values):
    return values * lax.rsqrt(jnp.mean(values * values, axis=-1, keepdims=True) + 1e-06)


def norm_pull(values, grads):
    scale = lax.rsqrt(jnp.mean(values * values, axis=-1, keepdims=True) + 1e-06)
    inner = jnp.mean(values * grads, axis=-1, keepdims=True)
    return scale * (grads - values * (inner * scale * scale))


def band(low_ref, proj_ref, high_ref, start, offset, size):
    return jnp.concatenate(
        [
            low_ref[:, start : start + size],
            proj_ref[:, offset + start : offset + start + size],
            high_ref[:, start : start + size],
        ],
        axis=0,
    )


def nt(a, b):
    return lax.dot_general(a, b, (((1,), (1,)), ((), ())), preferred_element_type=F32)


def nn(a, b):
    return lax.dot_general(a, b, (((1,), (0,)), ((), ())), preferred_element_type=F32)


def tn(a, b):
    return lax.dot_general(a, b, (((0,), (0,)), ((), ())), preferred_element_type=F32)


def spans(width, size):
    return [(start, start + size) for start in range(0, width, size)]


def softmax_band(proj_ref, keys, used, cuts, scale):
    scores = [nt(proj_ref[:, a:b], key) * scale for (a, b), key in zip(cuts, keys)]
    weights = [jnp.where(used, jnp.exp(score), 0.0) for score in scores]
    sums = [jnp.sum(weight, axis=-1, keepdims=True) for weight in weights]
    return [weight / total for weight, total in zip(weights, sums)]


def attend_kernel(state_ref, proj_ref, low_ref, high_ref, mask_ref, out_ref):
    width = state_ref.shape[1]
    size = width // HEADS
    cuts = spans(width, size)
    used = mask_ref[...] > 0
    keys = [band(low_ref, proj_ref, high_ref, a, width, size) for a, _ in cuts]
    values = [band(low_ref, proj_ref, high_ref, width + a, width, size) for a, _ in cuts]
    probs = softmax_band(proj_ref, keys, used, cuts, size ** (-0.5))
    mixed = [nn(p.astype(BF16), v) for p, v in zip(probs, values)]
    for (a, b), term in zip(cuts, mixed):
        out_ref[:, a:b] = (state_ref[:, a:b].astype(F32) + term).astype(BF16)


def attend(state, proj, low, high, mask):
    return pl.pallas_call(
        attend_kernel,
        out_shape=jax.ShapeDtypeStruct(state.shape, BF16),
        in_specs=[pl.BlockSpec(memory_space=pltpu.VMEM)] * 5,
        out_specs=pl.BlockSpec(memory_space=pltpu.VMEM),
        compiler_params=pltpu.CompilerParams(vmem_limit_bytes=KERNEL_VMEM),
        name="attend",
    )(state, proj, low, high, mask)


def pull_kernel(proj_ref, low_ref, high_ref, mask_ref, up_ref, query_ref, own_ref, low_out, high_out):
    width = up_ref.shape[1]
    size = width // HEADS
    rim = low_ref.shape[0]
    rows = proj_ref.shape[0]
    scale = size ** (-0.5)
    cuts = spans(width, size)
    used = mask_ref[...] > 0
    keys = [band(low_ref, proj_ref, high_ref, a, width, size) for a, _ in cuts]
    values = [band(low_ref, proj_ref, high_ref, width + a, width, size) for a, _ in cuts]
    probs = softmax_band(proj_ref, keys, used, cuts, scale)
    grad_probs = [nt(up_ref[:, a:b], v).astype(BF16).astype(F32) for (a, b), v in zip(cuts, values)]
    inner = [jnp.sum(g * p, axis=-1, keepdims=True) for g, p in zip(grad_probs, probs)]
    grad_scores = [
        (p * (g - i) * scale).astype(BF16) for p, g, i in zip(probs, grad_probs, inner)
    ]
    for (a, b), grad, key in zip(cuts, grad_scores, keys):
        query_ref[:, a:b] = nn(grad, key).astype(BF16)
    for base, left, right in (
        (0, grad_scores, proj_ref),
        (width, [p.astype(BF16) for p in probs], up_ref),
    ):
        for (a, b), rows_left in zip(cuts, left):
            grad = tn(rows_left, right[:, a:b])
            c, d = base + a, base + b
            low_out[:, c:d] = grad[:rim].astype(BF16)
            own_ref[:, c:d] = grad[rim : rim + rows]
            high_out[:, c:d] = grad[rim + rows :].astype(BF16)


def attend_pull(proj, low, high, mask, upstream):
    rows, width = upstream.shape
    rim = low.shape[0]
    return pl.pallas_call(
        pull_kernel,
        out_shape=(
            jax.ShapeDtypeStruct((rows, width), BF16),
            jax.ShapeDtypeStruct((rows, 2 * width), F32),
            jax.ShapeDtypeStruct((rim, 2 * width), BF16),
            jax.ShapeDtypeStruct((rim, 2 * width), BF16),
        ),
        in_specs=[pl.BlockSpec(memory_space=pltpu.VMEM)] * 5,
        out_specs=[pl.BlockSpec(memory_space=pltpu.VMEM)] * 4,
        compiler_params=pltpu.CompilerParams(vmem_limit_bytes=KERNEL_VMEM),
        name="attend_pull",
    )(proj, low, high, mask, upstream)


def route(obs_rows, obs_device, obs_node, encode_weight, node_state):
    micro, nodes_dev, width = node_state.shape
    per_dev, levels = obs_rows.shape[1:]
    node_devs = lax.axis_size(NODE)
    capacity = max(2, 2 * per_dev // node_devs)
    slots = node_devs * micro * capacity
    target = obs_device[..., 0]
    named = (target[..., None] == jnp.arange(node_devs)[None, None, :]).astype(BF16)
    earlier = (jnp.arange(per_dev)[:, None] > jnp.arange(per_dev)[None, :]).astype(BF16)
    before = jnp.einsum("ij,mjd->mid", earlier, named, preferred_element_type=F32)
    ranked = jnp.sum(before * named.astype(F32), axis=-1).astype(jnp.int32)
    position = (target * micro + jnp.arange(micro)[:, None]) * capacity + ranked
    chosen = (jnp.arange(slots)[:, None] == position.reshape(1, -1)).astype(BF16)
    payload = jnp.concatenate([obs_rows, obs_node[..., None].astype(BF16)], axis=-1)
    sent = nn(chosen, payload.reshape(micro * per_dev, levels + 1)).astype(BF16)
    received = lax.all_to_all(
        sent.reshape(node_devs, micro * capacity, levels + 1),
        NODE,
        split_axis=0,
        concat_axis=0,
        tiled=True,
    ).reshape(slots, levels + 1)
    owner = received[:, levels].astype(jnp.int32)
    owner = owner + (jnp.arange(slots) // capacity % micro) * nodes_dev
    held = (jnp.arange(micro * nodes_dev)[:, None] == owner[None, :]).astype(BF16)
    summed = nn(held, received[:, :levels])
    high = lax.reduce_precision(summed, 8, 7)
    rest = summed - high
    encoded = nn(high.astype(BF16), encode_weight) + nn(rest.astype(BF16), encode_weight)
    return (node_state.astype(F32) + encoded.reshape(micro, nodes_dev, width)).astype(BF16)


def body(
    master,
    first_moment,
    second_moment,
    node_state,
    obs_rows,
    obs_device,
    obs_node,
    encode_weight,
    decode_weight,
    neighbors,
    neighbor_count,
    out_grad,
):
    sections = lax.axis_size("section")
    section = lax.axis_index("section")
    node_devs = lax.axis_size(NODE)
    micro, nodes_dev, width = node_state.shape
    total_nodes = nodes_dev * node_devs
    anchor = lax.axis_index(NODE) * nodes_dev
    weight_full = lax.all_gather(master[0].astype(BF16), NODE, axis=0, tiled=True)
    entry = route(obs_rows, obs_device, obs_node, encode_weight, node_state)
    rim = HALO_W
    relative = (neighbors - anchor) % total_nodes
    relative = jnp.where(relative >= total_nodes - rim, relative - total_nodes, relative) + rim
    extent = nodes_dev + 2 * rim
    valid = jnp.arange(neighbors.shape[1])[None, :] < neighbor_count[:, None]
    at = (relative[..., None] == jnp.arange(extent)[None, None, :]) & valid[..., None]
    mask = jnp.sum(at.astype(F32), axis=1)

    ticks = micro + sections - 1
    incoming = jnp.zeros((nodes_dev, width), BF16)
    saved = []
    kept_normed = [jnp.zeros((nodes_dev, width), BF16)] * micro
    for tick in range(ticks):
        state = jnp.where(section == 0, entry[min(tick, micro - 1)], incoming)
        normed = norm_rows(state.astype(F32)).astype(BF16)
        proj = nn(normed, weight_full).astype(BF16)
        low = lax.ppermute(proj[nodes_dev - rim :, width:], NODE, ring(1))
        high = lax.ppermute(proj[:rim, width:], NODE, ring(-1))
        saved.append((state, proj, low, high))
        for batch in range(micro):
            kept_normed[batch] = jnp.where(section == tick - batch, normed, kept_normed[batch])
        if tick + 1 < ticks:
            incoming = from_behind(attend(state, proj, low, high, mask), "section", 1)
    normed_all = lax.all_gather(jnp.stack(kept_normed), PLANE, axis=0, tiled=False)

    head_grad = nt(out_grad.reshape(micro * nodes_dev, -1), decode_weight)
    head_grad = head_grad.astype(BF16).reshape(micro, nodes_dev, width)
    returning = jnp.zeros((nodes_dev, width), BF16)
    plane = lax.axis_size(PLANE)
    columns = 3 * width // plane
    kept_grad = [jnp.zeros((nodes_dev, 3 * width), BF16)] * micro
    for tick in range(ticks):
        sources = {}
        for stage in range(sections):
            batch = tick - (sections - 1) + stage
            if 0 <= batch < micro:
                sources[stage] = (batch, batch + stage)
        stages = sorted(sources)
        state, proj, low, high = saved[sources[stages[0]][1]]
        for stage in stages[1:]:
            here = section == stage
            state, proj, low, high = (
                jnp.where(here, a, b)
                for a, b in zip(saved[sources[stage][1]], (state, proj, low, high))
            )
        upstream = returning
        if sections - 1 in sources:
            upstream = jnp.where(
                section == sections - 1, head_grad[sources[sections - 1][0]], returning
            )
        grad_query, own, low_edge, high_edge = attend_pull(proj, low, high, mask, upstream)
        from_low = lax.ppermute(high_edge, NODE, ring(1))
        from_high = lax.ppermute(low_edge, NODE, ring(-1))
        own = own + jnp.concatenate([from_low, from_high], axis=0).astype(F32)
        grad_qkv = jnp.concatenate([grad_query, own.astype(BF16)], axis=1)
        for stage in stages:
            batch = sources[stage][0]
            kept_grad[batch] = jnp.where(section == stage, grad_qkv, kept_grad[batch])
        if tick + 1 < ticks:
            grad_normed = nt(grad_qkv, weight_full)
            downward = (upstream.astype(F32) + norm_pull(state.astype(F32), grad_normed)).astype(
                BF16
            )
            returning = from_behind(downward, "section", -1)
    parts = jnp.concatenate(kept_grad, axis=0).reshape(micro * nodes_dev, plane, columns)
    gathered = lax.all_to_all(
        parts.transpose(1, 0, 2), PLANE, split_axis=0, concat_axis=0, tiled=True
    )
    partial = tn(
        normed_all.reshape(plane * micro * nodes_dev, width),
        gathered.reshape(plane * micro * nodes_dev, columns),
    )
    rows = width // node_devs
    pieces = lax.all_to_all(
        partial.astype(BF16).reshape(node_devs, rows, columns),
        NODE,
        split_axis=0,
        concat_axis=0,
        tiled=True,
    )
    pieces = pieces.reshape(node_devs // plane, plane, rows, columns).astype(F32)
    gradient = jnp.sum(pieces, axis=0).transpose(1, 0, 2).reshape(1, rows, 3 * width)
    new_first = BETA_ONE * first_moment + (1.0 - BETA_ONE) * gradient
    new_second = BETA_TWO * second_moment + (1.0 - BETA_TWO) * gradient * gradient
    step_size = (
        new_first / (1.0 - BETA_ONE**STEP) / (jnp.sqrt(new_second / (1.0 - BETA_TWO**STEP)) + 1e-08)
    )
    new_weights = master - LEARN_RATE * step_size
    return (new_weights, new_first, new_second)


def solution(mesh):
    sections, node_devs = mesh.devices.shape
    fine = Mesh(mesh.devices.reshape(sections, node_devs // 8, 4, 2), ("section",) + NODE)
    in_specs = (
        P("section", NODE, None),
        P("section", NODE, None),
        P("section", NODE, None),
        P(None, NODE, None),
        P(None, NODE, None),
        P(None, NODE, None),
        P(None, NODE),
        P(),
        P(),
        P(NODE, None),
        P(NODE),
        P(None, NODE, None),
    )
    out_specs = (P("section", NODE, None), P("section", NODE, None), P("section", NODE, None))
    return jax.shard_map(body, mesh=fine, in_specs=in_specs, out_specs=out_specs, check_vma=False)
```

```python
import jax
import jax.numpy as jnp
from jax import lax
from jax.experimental import pallas as pl
from jax.experimental.pallas import tpu as pltpu
from jax.sharding import Mesh, PartitionSpec as P

HEADS = 8
HALO_W = 32
STEP = 100


BETA_ONE = 0.9
BETA_TWO = 0.999
LEARN_RATE = 0.001

NODE = ("z", "x", "core")
PLANE = ("x", "core")
F32 = jnp.float32
BF16 = jnp.bfloat16
KERNEL_VMEM = 12 * 2**20


def across(index, count):
    return (index + 1) % count if index % 2 else (index - 1) % count


def swap(value):
    return lax.ppermute(value, "core", [(0, 1), (1, 0)])


def beside(value, steps):
    sections, count = lax.axis_size("section"), lax.axis_size(NODE)
    moves = [
        (section * count + index, (section + steps) * count + across(index, count))
        for section in range(sections)
        if 0 <= section + steps < sections
        for index in range(count)
    ]
    return lax.ppermute(value, ("section",) + NODE, moves)


def from_behind(value, axis, steps):
    count = lax.axis_size(axis)
    leading, last = (max(0, -steps), min(count, count - steps))
    return lax.ppermute(value, axis, [(source, source + steps) for source in range(leading, last)])


def norm_rows(values):
    return values * lax.rsqrt(jnp.mean(values * values, axis=-1, keepdims=True) + 1e-06)


def norm_pull(values, grads):
    scale = lax.rsqrt(jnp.mean(values * values, axis=-1, keepdims=True) + 1e-06)
    inner = jnp.mean(values * grads, axis=-1, keepdims=True)
    return scale * (grads - values * (inner * scale * scale))


def nt(a, b):
    return lax.dot_general(a, b, (((1,), (1,)), ((), ())), preferred_element_type=F32)


def nn(a, b):
    return lax.dot_general(a, b, (((1,), (0,)), ((), ())), preferred_element_type=F32)


def tn(a, b):
    return lax.dot_general(a, b, (((0,), (0,)), ((), ())), preferred_element_type=F32)


def spans(width, size):
    return [(start, start + size) for start in range(0, width, size)]


def rows_of(*pieces):
    return jnp.concatenate(pieces, axis=0)


def softmax_band(queries, keys, used, scale):
    scores = [nt(query, key) * scale for query, key in zip(queries, keys)]
    weights = [jnp.where(u, jnp.exp(score), 0.0) for u, score in zip(used, scores)]
    sums = [jnp.sum(weight, axis=-1, keepdims=True) for weight in weights]
    return [weight / total for weight, total in zip(weights, sums)]


def attend_kernel(side_ref, state_ref, proj_ref, mask_ref, out_ref):
    rows, width = state_ref.shape
    size = width // HEADS
    cuts = spans(width, size)
    half = rows // 2
    below = 2 - side_ref[0]
    above = 3 - below
    used = [mask_ref[...] > 0] * HEADS

    def banded(base):
        return [
            rows_of(
                proj_ref[below, half:, base + a : base + b],
                proj_ref[0, :, base + a : base + b],
                proj_ref[above, :half, base + a : base + b],
            )
            for a, b in cuts
        ]

    queries = [proj_ref[0, :, a:b] for a, b in cuts]
    probs = softmax_band(queries, banded(width), used, size ** (-0.5))
    mixed = [nn(p.astype(BF16), v) for p, v in zip(probs, banded(2 * width))]
    for (a, b), term in zip(cuts, mixed):
        out_ref[:, a:b] = (state_ref[:, a:b].astype(F32) + term).astype(BF16)


VMEM = pl.BlockSpec(memory_space=pltpu.VMEM)
SMEM = pl.BlockSpec(memory_space=pltpu.SMEM)


def attend(side, state, proj, mask):
    return pl.pallas_call(
        attend_kernel,
        out_shape=jax.ShapeDtypeStruct(state.shape, BF16),
        in_specs=[SMEM, VMEM, VMEM, VMEM],
        out_specs=VMEM,
        compiler_params=pltpu.CompilerParams(vmem_limit_bytes=KERNEL_VMEM),
        name="attend",
    )(side, state, proj, mask)


def pull_kernel(side_ref, proj_ref, mask_ref, own_ref, edge_ref, out_ref):
    rows, width = own_ref.shape
    size = width // HEADS
    scale = size ** (-0.5)
    cuts = spans(width, size)
    half = rows // 2
    below = 2 - side_ref[0]
    above = 3 - below

    def low_queries(a, b):
        return rows_of(proj_ref[below, half:, a:b], proj_ref[0, :half, a:b])

    def high_queries(a, b):
        return rows_of(proj_ref[0, half:, a:b], proj_ref[above, :half, a:b])

    def low_keys(a, b):
        return rows_of(proj_ref[below, :, a:b], proj_ref[0, :, a:b])

    def high_keys(a, b):
        return rows_of(proj_ref[0, :, a:b], proj_ref[above, :, a:b])

    def both(low, high, base):
        return [low(base + a, base + b) for a, b in cuts] + [
            high(base + a, base + b) for a, b in cuts
        ]

    queries = both(low_queries, high_queries, 0)
    keys = both(low_keys, high_keys, width)
    values = both(low_keys, high_keys, 2 * width)
    upstream = [rows_of(edge_ref[below - 1, :, a:b], own_ref[:half, a:b]) for a, b in cuts] + [
        rows_of(own_ref[half:, a:b], edge_ref[above - 1, :, a:b]) for a, b in cuts
    ]
    used = [mask_ref[0] > 0] * HEADS + [mask_ref[1] > 0] * HEADS
    probs = softmax_band(queries, keys, used, scale)
    grad_probs = [nt(u, v).astype(BF16).astype(F32) for u, v in zip(upstream, values)]
    inner = [jnp.sum(g * p, axis=-1, keepdims=True) for g, p in zip(grad_probs, probs)]
    grad_scores = [
        (p * (g - i) * scale).astype(BF16) for p, g, i in zip(probs, grad_probs, inner)
    ]
    rounded = [p.astype(BF16) for p in probs]
    for head, (a, b) in enumerate(cuts):
        low, high = head, HEADS + head
        out_ref[:half, a:b] = nn(grad_scores[low], keys[low])[half:].astype(BF16)
        out_ref[half:, a:b] = nn(grad_scores[high], keys[high])[:half].astype(BF16)
        for base, left, right in ((width, grad_scores, queries), (2 * width, rounded, upstream)):
            total = tn(left[low], right[low])[rows:] + tn(left[high], right[high])[:rows]
            out_ref[:, base + a : base + b] = total.astype(BF16)


def attend_pull(side, proj, masks, own, edges):
    return pl.pallas_call(
        pull_kernel,
        out_shape=jax.ShapeDtypeStruct(proj.shape[1:], BF16),
        in_specs=[SMEM, VMEM, VMEM, VMEM, VMEM],
        out_specs=VMEM,
        compiler_params=pltpu.CompilerParams(vmem_limit_bytes=KERNEL_VMEM),
        name="attend_pull",
    )(side, proj, masks, own, edges)


def route(obs_rows, obs_device, obs_node, encode_weight, node_state):
    micro, nodes_dev, width = node_state.shape
    per_dev, levels = obs_rows.shape[1:]
    node_devs = lax.axis_size(NODE)
    capacity = max(2, 2 * per_dev // node_devs)
    slots = node_devs * micro * capacity
    target = obs_device[..., 0]
    named = (target[..., None] == jnp.arange(node_devs)[None, None, :]).astype(BF16)
    earlier = (jnp.arange(per_dev)[:, None] > jnp.arange(per_dev)[None, :]).astype(BF16)
    before = jnp.einsum("ij,mjd->mid", earlier, named, preferred_element_type=F32)
    ranked = jnp.sum(before * named.astype(F32), axis=-1).astype(jnp.int32)
    position = (target * micro + jnp.arange(micro)[:, None]) * capacity + ranked
    chosen = (jnp.arange(slots)[:, None] == position.reshape(1, -1)).astype(BF16)
    payload = jnp.concatenate([obs_rows, obs_node[..., None].astype(BF16)], axis=-1)
    sent = nn(chosen, payload.reshape(micro * per_dev, levels + 1)).astype(BF16)
    received = lax.all_to_all(
        sent.reshape(node_devs, micro * capacity, levels + 1),
        NODE,
        split_axis=0,
        concat_axis=0,
        tiled=True,
    ).reshape(slots, levels + 1)
    owner = received[:, levels].astype(jnp.int32)
    owner = owner + (jnp.arange(slots) // capacity % micro) * nodes_dev
    held = (jnp.arange(micro * nodes_dev)[:, None] == owner[None, :]).astype(BF16)
    summed = nn(held, received[:, :levels])
    high = lax.reduce_precision(summed, 8, 7)
    rest = summed - high
    encoded = nn(high.astype(BF16), encode_weight) + nn(rest.astype(BF16), encode_weight)
    return (node_state.astype(F32) + encoded.reshape(micro, nodes_dev, width)).astype(BF16)


def body(
    master,
    first_moment,
    second_moment,
    node_state,
    obs_rows,
    obs_device,
    obs_node,
    encode_weight,
    decode_weight,
    neighbors,
    neighbor_count,
    out_grad,
):
    sections = lax.axis_size("section")
    section = lax.axis_index("section")
    node_devs = lax.axis_size(NODE)
    micro, nodes_dev, width = node_state.shape
    total_nodes = nodes_dev * node_devs
    anchor = lax.axis_index(NODE) * nodes_dev
    weight_full = lax.all_gather(master[0].astype(BF16), NODE, axis=0, tiled=True)
    core = lax.axis_index("core")
    side = core.astype(jnp.int32).reshape(1)
    half = nodes_dev // 2

    def pair_edge(value):
        return jnp.where(core == 0, value[..., half:, :], value[..., :half, :])

    def cross_edge(value):
        return jnp.where(core == 0, value[..., :half, :], value[..., half:, :])

    entry = route(obs_rows, obs_device, obs_node, encode_weight, node_state)
    rim = HALO_W
    relative = (neighbors - anchor) % total_nodes
    relative = jnp.where(relative >= total_nodes - rim, relative - total_nodes, relative) + rim
    relative = relative - half * (jnp.arange(nodes_dev)[:, None] // half)
    reach = half + 2 * rim
    valid = jnp.arange(neighbors.shape[1])[None, :] < neighbor_count[:, None]
    at = (relative[..., None] == jnp.arange(reach)[None, None, :]) & valid[..., None]
    near = jnp.sum(at.astype(F32), axis=1).astype(BF16)
    head_grad = nt(out_grad.reshape(micro * nodes_dev, -1), decode_weight)
    head_grad = head_grad.astype(BF16).reshape(micro, nodes_dev, width)

    def packed(edge):
        return jnp.concatenate(
            [edge(head_grad).reshape(-1, width), jnp.pad(edge(near), ((0, 0), (0, width - reach)))]
        )

    from_pair = swap(packed(pair_edge))
    from_cross = beside(jnp.concatenate([packed(cross_edge), entry.reshape(-1, width)]), 0)
    entry, from_pair, from_cross, head_grad = lax.optimization_barrier(
        (entry, from_pair, from_cross, head_grad)
    )
    heads = micro * half
    head_pair = from_pair[:heads].reshape(micro, half, width)
    head_cross = from_cross[:heads].reshape(micro, half, width)
    near_pair = from_pair[heads : heads + half, :reach]
    near_cross = from_cross[heads : heads + half, :reach]
    entry_cross = from_cross[heads + half :].reshape(micro, nodes_dev, width)
    near_low = jnp.where(core == 0, near_cross, near_pair)
    near_high = jnp.where(core == 0, near_pair, near_cross)

    def bands(upper, lower):
        room = 2 * nodes_dev - reach
        return jnp.concatenate(
            [jnp.pad(upper, ((0, 0), (0, room))), jnp.pad(lower, ((0, 0), (room, 0)))]
        ).astype(F32)

    mask = bands(near[:half], near[half:])
    masks = jnp.stack([bands(near_low, near[:half]), bands(near[half:], near_high)])

    ticks = micro + sections - 1
    incoming, incoming_cross = None, None
    saved = []
    kept_normed = [None] * micro
    for tick in range(ticks):
        state, cross = incoming, incoming_cross
        if tick == 0:
            state, cross = entry[0], entry_cross[0]
        elif tick < micro:
            state = jnp.where(section == 0, entry[tick], incoming)
            cross = jnp.where(section == 0, entry_cross[tick], incoming_cross)
        around = jnp.concatenate([state, swap(state), cross], axis=0)
        normed = norm_rows(around.astype(F32)).astype(BF16)
        proj = nn(normed, weight_full).astype(BF16).reshape(3, nodes_dev, 3 * width)
        saved.append((state, proj))
        for batch in range(micro):
            stage = tick - batch
            if stage == 0:
                kept_normed[batch] = normed[:nodes_dev]
            elif 0 < stage < sections:
                kept_normed[batch] = jnp.where(
                    section == stage, normed[:nodes_dev], kept_normed[batch]
                )
        if tick + 1 < ticks:
            output = attend(side, state, proj, mask)
            incoming_cross = beside(output, 1)
            incoming = from_behind(output, "section", 1)
    normed_all = lax.all_gather(jnp.stack(kept_normed), PLANE, axis=0, tiled=False)

    returning, returning_cross = None, None
    plane = lax.axis_size(PLANE)
    columns = 3 * width // plane
    kept_grad = [None] * micro
    for tick in range(ticks):
        sources = {}
        for stage in range(sections):
            batch = tick - (sections - 1) + stage
            if 0 <= batch < micro:
                sources[stage] = (batch, batch + stage)
        stages = sorted(sources)
        state, proj = saved[sources[stages[0]][1]]
        for stage in stages[1:]:
            here = section == stage
            state, proj = (
                jnp.where(here, a, b) for a, b in zip(saved[sources[stage][1]], (state, proj))
            )
        last = sections - 1
        if last not in sources:
            own, pair, cross = returning, swap(pair_edge(returning)), returning_cross
        elif tick == 0:
            own, pair, cross = head_grad[0], head_pair[0], head_cross[0]
        else:
            batch = sources[last][0]
            own = jnp.where(section == last, head_grad[batch], returning)
            cross = jnp.where(section == last, head_cross[batch], returning_cross)
            pair = swap(pair_edge(own))
        grad_qkv = attend_pull(side, proj, masks, own, jnp.stack([pair, cross]))
        for stage in stages:
            batch = sources[stage][0]
            if kept_grad[batch] is None:
                kept_grad[batch] = grad_qkv
            else:
                kept_grad[batch] = jnp.where(section == stage, grad_qkv, kept_grad[batch])
        if tick + 1 < ticks:
            grad_normed = nt(grad_qkv, weight_full)
            downward = (own.astype(F32) + norm_pull(state.astype(F32), grad_normed)).astype(BF16)
            returning_cross = beside(cross_edge(downward), -1)
            returning = from_behind(downward, "section", -1)
    parts = jnp.concatenate(kept_grad, axis=0).reshape(micro * nodes_dev, plane, columns)
    gathered = lax.all_to_all(
        parts.transpose(1, 0, 2), PLANE, split_axis=0, concat_axis=0, tiled=True
    )
    partial = tn(
        normed_all.reshape(plane * micro * nodes_dev, width),
        gathered.reshape(plane * micro * nodes_dev, columns),
    )
    rows = width // node_devs
    pieces = lax.all_to_all(
        partial.astype(BF16).reshape(node_devs, rows, columns),
        NODE,
        split_axis=0,
        concat_axis=0,
        tiled=True,
    )
    pieces = pieces.reshape(node_devs // plane, plane, rows, columns).astype(F32)
    gradient = jnp.sum(pieces, axis=0).transpose(1, 0, 2).reshape(1, rows, 3 * width)
    new_first = BETA_ONE * first_moment + (1.0 - BETA_ONE) * gradient
    new_second = BETA_TWO * second_moment + (1.0 - BETA_TWO) * gradient * gradient
    step_size = (
        new_first / (1.0 - BETA_ONE**STEP) / (jnp.sqrt(new_second / (1.0 - BETA_TWO**STEP)) + 1e-08)
    )
    new_weights = master - LEARN_RATE * step_size
    return (new_weights, new_first, new_second)


def solution(mesh):
    sections, node_devs = mesh.devices.shape
    fine = Mesh(mesh.devices.reshape(sections, node_devs // 8, 4, 2), ("section",) + NODE)
    in_specs = (
        P("section", NODE, None),
        P("section", NODE, None),
        P("section", NODE, None),
        P(None, NODE, None),
        P(None, NODE, None),
        P(None, NODE, None),
        P(None, NODE),
        P(),
        P(),
        P(NODE, None),
        P(NODE),
        P(None, NODE, None),
    )
    out_specs = (P("section", NODE, None), P("section", NODE, None), P("section", NODE, None))
    return jax.shard_map(body, mesh=fine, in_specs=in_specs, out_specs=out_specs, check_vma=False)
```

```python
import jax
import jax.numpy as jnp
from jax import lax
from jax.experimental import pallas as pl
from jax.experimental.pallas import tpu as pltpu
from jax.sharding import Mesh, PartitionSpec as P

HEADS = 8
HALO_W = 32
STEP = 100


BETA_ONE = 0.9
BETA_TWO = 0.999
LEARN_RATE = 0.001

NODE = ("z", "x", "core")
PLANE = ("x", "core")
F32 = jnp.float32
BF16 = jnp.bfloat16
KERNEL_VMEM = 12 * 2**20


def across(index, count):
    return (index + 1) % count if index % 2 else (index - 1) % count


def swap(value):
    return lax.ppermute(value, "core", [(0, 1), (1, 0)])


def beside(value, steps):
    sections, count = lax.axis_size("section"), lax.axis_size(NODE)
    moves = [
        (section * count + index, (section + steps) * count + across(index, count))
        for section in range(sections)
        if 0 <= section + steps < sections
        for index in range(count)
    ]
    return lax.ppermute(value, ("section",) + NODE, moves)


def from_behind(value, axis, steps):
    count = lax.axis_size(axis)
    leading, last = (max(0, -steps), min(count, count - steps))
    return lax.ppermute(value, axis, [(source, source + steps) for source in range(leading, last)])


def norm_rows(values):
    return values * lax.rsqrt(jnp.mean(values * values, axis=-1, keepdims=True) + 1e-06)


def norm_pull(values, grads):
    scale = lax.rsqrt(jnp.mean(values * values, axis=-1, keepdims=True) + 1e-06)
    inner = jnp.mean(values * grads, axis=-1, keepdims=True)
    return scale * (grads - values * (inner * scale * scale))


def nt(a, b):
    return lax.dot_general(a, b, (((1,), (1,)), ((), ())), preferred_element_type=F32)


def nn(a, b):
    return lax.dot_general(a, b, (((1,), (0,)), ((), ())), preferred_element_type=F32)


def tn(a, b):
    return lax.dot_general(a, b, (((0,), (0,)), ((), ())), preferred_element_type=F32)


def spans(width, size):
    return [(start, start + size) for start in range(0, width, size)]


def rows_of(*pieces):
    return jnp.concatenate(pieces, axis=0)


def softmax_band(queries, keys, used, scale):
    scores = [nt(query, key) * scale for query, key in zip(queries, keys)]
    weights = [jnp.where(u, jnp.exp(score), 0.0) for u, score in zip(used, scores)]
    sums = [jnp.sum(weight, axis=-1, keepdims=True) for weight in weights]
    return [weight / total for weight, total in zip(weights, sums)]


def attend_kernel(side_ref, state_ref, proj_ref, mask_ref, out_ref):
    rows, width = state_ref.shape
    size = width // HEADS
    cuts = spans(width, size)
    half = rows // 2
    below = 2 - side_ref[0]
    above = 3 - below
    used = [mask_ref[...] > 0] * HEADS

    def banded(base):
        return [
            rows_of(
                proj_ref[below, half:, base + a : base + b],
                proj_ref[0, :, base + a : base + b],
                proj_ref[above, :half, base + a : base + b],
            )
            for a, b in cuts
        ]

    queries = [proj_ref[0, :, a:b] for a, b in cuts]
    probs = softmax_band(queries, banded(width), used, size ** (-0.5))
    mixed = [nn(p.astype(BF16), v) for p, v in zip(probs, banded(2 * width))]
    for (a, b), term in zip(cuts, mixed):
        out_ref[:, a:b] = (state_ref[:, a:b].astype(F32) + term).astype(BF16)


VMEM = pl.BlockSpec(memory_space=pltpu.VMEM)
SMEM = pl.BlockSpec(memory_space=pltpu.SMEM)


def attend(side, state, proj, mask):
    return pl.pallas_call(
        attend_kernel,
        out_shape=jax.ShapeDtypeStruct(state.shape, BF16),
        in_specs=[SMEM, VMEM, VMEM, VMEM],
        out_specs=VMEM,
        compiler_params=pltpu.CompilerParams(vmem_limit_bytes=KERNEL_VMEM),
        name="attend",
    )(side, state, proj, mask)


def pull_kernel(side_ref, proj_ref, mask_ref, own_ref, edge_ref, out_ref):
    rows, width = own_ref.shape
    size = width // HEADS
    scale = size ** (-0.5)
    cuts = spans(width, size)
    half = rows // 2
    below = 2 - side_ref[0]
    above = 3 - below

    def low_queries(a, b):
        return rows_of(proj_ref[below, half:, a:b], proj_ref[0, :half, a:b])

    def high_queries(a, b):
        return rows_of(proj_ref[0, half:, a:b], proj_ref[above, :half, a:b])

    def low_keys(a, b):
        return rows_of(proj_ref[below, :, a:b], proj_ref[0, :, a:b])

    def high_keys(a, b):
        return rows_of(proj_ref[0, :, a:b], proj_ref[above, :, a:b])

    def both(low, high, base):
        return [low(base + a, base + b) for a, b in cuts] + [
            high(base + a, base + b) for a, b in cuts
        ]

    queries = both(low_queries, high_queries, 0)
    keys = both(low_keys, high_keys, width)
    values = both(low_keys, high_keys, 2 * width)
    upstream = [rows_of(edge_ref[below - 1, :, a:b], own_ref[:half, a:b]) for a, b in cuts] + [
        rows_of(own_ref[half:, a:b], edge_ref[above - 1, :, a:b]) for a, b in cuts
    ]
    used = [mask_ref[0] > 0] * HEADS + [mask_ref[1] > 0] * HEADS
    probs = softmax_band(queries, keys, used, scale)
    grad_probs = [nt(u, v).astype(BF16).astype(F32) for u, v in zip(upstream, values)]
    inner = [jnp.sum(g * p, axis=-1, keepdims=True) for g, p in zip(grad_probs, probs)]
    grad_scores = [
        (p * (g - i) * scale).astype(BF16) for p, g, i in zip(probs, grad_probs, inner)
    ]
    rounded = [p.astype(BF16) for p in probs]
    for head, (a, b) in enumerate(cuts):
        low, high = head, HEADS + head
        out_ref[:half, a:b] = nn(grad_scores[low], keys[low])[half:].astype(BF16)
        out_ref[half:, a:b] = nn(grad_scores[high], keys[high])[:half].astype(BF16)
        for base, left, right in ((width, grad_scores, queries), (2 * width, rounded, upstream)):
            total = tn(left[low], right[low])[rows:] + tn(left[high], right[high])[:rows]
            out_ref[:, base + a : base + b] = total.astype(BF16)


def attend_pull(side, proj, masks, own, edges):
    return pl.pallas_call(
        pull_kernel,
        out_shape=jax.ShapeDtypeStruct(proj.shape[1:], BF16),
        in_specs=[SMEM, VMEM, VMEM, VMEM, VMEM],
        out_specs=VMEM,
        compiler_params=pltpu.CompilerParams(vmem_limit_bytes=KERNEL_VMEM),
        name="attend_pull",
    )(side, proj, masks, own, edges)


def route(obs_rows, obs_device, obs_node, encode_weight, node_state):
    micro, nodes_dev, width = node_state.shape
    per_dev, levels = obs_rows.shape[1:]
    node_devs = lax.axis_size(NODE)
    capacity = max(2, 2 * per_dev // node_devs)
    slots = node_devs * micro * capacity
    target = obs_device[..., 0]
    named = (target[..., None] == jnp.arange(node_devs)[None, None, :]).astype(BF16)
    earlier = (jnp.arange(per_dev)[:, None] > jnp.arange(per_dev)[None, :]).astype(BF16)
    before = jnp.einsum("ij,mjd->mid", earlier, named, preferred_element_type=F32)
    ranked = jnp.sum(before * named.astype(F32), axis=-1).astype(jnp.int32)
    position = (target * micro + jnp.arange(micro)[:, None]) * capacity + ranked
    chosen = (jnp.arange(slots)[:, None] == position.reshape(1, -1)).astype(BF16)
    payload = jnp.concatenate([obs_rows, obs_node[..., None].astype(BF16)], axis=-1)
    sent = nn(chosen, payload.reshape(micro * per_dev, levels + 1)).astype(BF16)
    received = lax.all_to_all(
        sent.reshape(node_devs, micro * capacity, levels + 1),
        NODE,
        split_axis=0,
        concat_axis=0,
        tiled=True,
    ).reshape(slots, levels + 1)
    owner = received[:, levels].astype(jnp.int32)
    owner = owner + (jnp.arange(slots) // capacity % micro) * nodes_dev
    held = (jnp.arange(micro * nodes_dev)[:, None] == owner[None, :]).astype(BF16)
    summed = nn(held, received[:, :levels])
    high = lax.reduce_precision(summed, 8, 7)
    rest = summed - high
    encoded = nn(high.astype(BF16), encode_weight) + nn(rest.astype(BF16), encode_weight)
    return (node_state.astype(F32) + encoded.reshape(micro, nodes_dev, width)).astype(BF16)


def body(
    master,
    first_moment,
    second_moment,
    node_state,
    obs_rows,
    obs_device,
    obs_node,
    encode_weight,
    decode_weight,
    neighbors,
    neighbor_count,
    out_grad,
):
    sections = lax.axis_size("section")
    section = lax.axis_index("section")
    node_devs = lax.axis_size(NODE)
    micro, nodes_dev, width = node_state.shape
    total_nodes = nodes_dev * node_devs
    anchor = lax.axis_index(NODE) * nodes_dev
    plane = lax.axis_size(PLANE)
    weight_rows = master.shape[1]
    weight_full = lax.all_gather(master[0].astype(BF16), "z", axis=0, tiled=True)
    weight_full = lax.all_gather(weight_full, PLANE, axis=0, tiled=True)
    weight_full = weight_full.reshape(plane, node_devs // plane, weight_rows, 3 * width)
    weight_full = weight_full.transpose(1, 0, 2, 3).reshape(width, 3 * width)
    core = lax.axis_index("core")
    side = core.astype(jnp.int32).reshape(1)
    half = nodes_dev // 2

    def pair_edge(value, first):
        return jnp.where(first, value[..., half:, :], value[..., :half, :])

    def cross_edge(value, first):
        return jnp.where(first, value[..., :half, :], value[..., half:, :])

    entry = route(obs_rows, obs_device, obs_node, encode_weight, node_state)
    rim = HALO_W
    relative = (neighbors - anchor) % total_nodes
    relative = jnp.where(relative >= total_nodes - rim, relative - total_nodes, relative) + rim
    relative = relative - half * (jnp.arange(nodes_dev)[:, None] // half)
    reach = half + 2 * rim
    valid = jnp.arange(neighbors.shape[1])[None, :] < neighbor_count[:, None]
    at = (relative[..., None] == jnp.arange(reach)[None, None, :]) & valid[..., None]
    near = jnp.sum(at.astype(F32), axis=1).astype(BF16)
    head_grad = nt(out_grad.reshape(micro * nodes_dev, -1), decode_weight)
    head_grad = head_grad.astype(BF16).reshape(micro, nodes_dev, width)

    def packed(edge):
        return jnp.concatenate(
            [
                edge(head_grad, core == 0).reshape(-1, width),
                jnp.pad(edge(near, core == 0), ((0, 0), (0, width - reach))),
            ]
        )

    from_pair = swap(packed(pair_edge))
    from_cross = beside(jnp.concatenate([packed(cross_edge), entry.reshape(-1, width)]), 0)
    at_stage = [section == stage for stage in range(sections)]
    entry, from_pair, from_cross, head_grad, first_core, side, at_stage = lax.optimization_barrier(
        (entry, from_pair, from_cross, head_grad, core == 0, side, at_stage)
    )
    heads = micro * half
    head_pair = from_pair[:heads].reshape(micro, half, width)
    head_cross = from_cross[:heads].reshape(micro, half, width)
    near_pair = from_pair[heads : heads + half, :reach]
    near_cross = from_cross[heads : heads + half, :reach]
    entry_cross = from_cross[heads + half :].reshape(micro, nodes_dev, width)
    near_low = jnp.where(first_core, near_cross, near_pair)
    near_high = jnp.where(first_core, near_pair, near_cross)

    def bands(upper, lower):
        room = 2 * nodes_dev - reach
        return jnp.concatenate(
            [jnp.pad(upper, ((0, 0), (0, room))), jnp.pad(lower, ((0, 0), (room, 0)))]
        ).astype(F32)

    mask = bands(near[:half], near[half:])
    masks = jnp.stack([bands(near_low, near[:half]), bands(near[half:], near_high)])

    ticks = micro + sections - 1
    incoming, incoming_cross = None, None
    saved = []
    kept_normed = [None] * micro
    for tick in range(ticks):
        state, cross = incoming, incoming_cross
        if tick == 0:
            state, cross = entry[0], entry_cross[0]
        elif tick < micro:
            state = jnp.where(at_stage[0], entry[tick], incoming)
            cross = jnp.where(at_stage[0], entry_cross[tick], incoming_cross)
        around = jnp.concatenate([state, swap(state), cross], axis=0)
        normed = norm_rows(around.astype(F32)).astype(BF16)
        proj = nn(normed, weight_full).astype(BF16).reshape(3, nodes_dev, 3 * width)
        saved.append((state, proj))
        for batch in range(micro):
            stage = tick - batch
            if stage == 0:
                kept_normed[batch] = normed[:nodes_dev]
            elif 0 < stage < sections:
                kept_normed[batch] = jnp.where(
                    at_stage[stage], normed[:nodes_dev], kept_normed[batch]
                )
        if tick + 1 < ticks:
            output = attend(side, state, proj, mask)
            incoming_cross = beside(output, 1)
            incoming = from_behind(output, "section", 1)
    returning, returning_cross = None, None
    columns = 3 * width // plane
    kept_grad = [None] * micro
    for tick in range(ticks):
        sources = {}
        for stage in range(sections):
            batch = tick - (sections - 1) + stage
            if 0 <= batch < micro:
                sources[stage] = (batch, batch + stage)
        stages = sorted(sources)
        state, proj = saved[sources[stages[0]][1]]
        for stage in stages[1:]:
            here = at_stage[stage]
            state, proj = (
                jnp.where(here, a, b) for a, b in zip(saved[sources[stage][1]], (state, proj))
            )
        last = sections - 1
        if last not in sources:
            own, pair, cross = returning, swap(pair_edge(returning, first_core)), returning_cross
        elif tick == 0:
            own, pair, cross = head_grad[0], head_pair[0], head_cross[0]
        else:
            batch = sources[last][0]
            own = jnp.where(at_stage[last], head_grad[batch], returning)
            cross = jnp.where(at_stage[last], head_cross[batch], returning_cross)
            pair = swap(pair_edge(own, first_core))
        grad_qkv = attend_pull(side, proj, masks, own, jnp.stack([pair, cross]))
        for stage in stages:
            batch = sources[stage][0]
            if kept_grad[batch] is None:
                kept_grad[batch] = grad_qkv
            else:
                kept_grad[batch] = jnp.where(at_stage[stage], grad_qkv, kept_grad[batch])
        if tick + 1 < ticks:
            grad_normed = nt(grad_qkv, weight_full)
            if tick + 2 == ticks:
                kept, grad_normed = lax.optimization_barrier((jnp.stack(kept_normed), grad_normed))
                normed_all = lax.all_gather(kept, PLANE, axis=0, tiled=False)
            downward = (own.astype(F32) + norm_pull(state.astype(F32), grad_normed)).astype(BF16)
            returning_cross = beside(cross_edge(downward, first_core), -1)
            returning = from_behind(downward, "section", -1)
    parts = jnp.concatenate(kept_grad, axis=0).reshape(micro * nodes_dev, plane, columns)
    gathered = lax.all_to_all(
        parts.transpose(1, 0, 2), PLANE, split_axis=0, concat_axis=0, tiled=True
    )
    partial = tn(
        normed_all.reshape(plane * micro * nodes_dev, width),
        gathered.reshape(plane * micro * nodes_dev, columns),
    )
    rows = width // node_devs
    pieces = lax.all_to_all(
        partial.astype(BF16).reshape(node_devs, rows, columns),
        NODE,
        split_axis=0,
        concat_axis=0,
        tiled=True,
    )
    pieces = pieces.reshape(node_devs // plane, plane, rows, columns).astype(F32)
    gradient = jnp.sum(pieces, axis=0).transpose(1, 0, 2).reshape(1, rows, 3 * width)
    new_first = BETA_ONE * first_moment + (1.0 - BETA_ONE) * gradient
    new_second = BETA_TWO * second_moment + (1.0 - BETA_TWO) * gradient * gradient
    step_size = (
        new_first / (1.0 - BETA_ONE**STEP) / (jnp.sqrt(new_second / (1.0 - BETA_TWO**STEP)) + 1e-08)
    )
    new_weights = master - LEARN_RATE * step_size
    return (new_weights, new_first, new_second)


def solution(mesh):
    sections, node_devs = mesh.devices.shape
    fine = Mesh(mesh.devices.reshape(sections, node_devs // 8, 4, 2), ("section",) + NODE)
    in_specs = (
        P("section", NODE, None),
        P("section", NODE, None),
        P("section", NODE, None),
        P(None, NODE, None),
        P(None, NODE, None),
        P(None, NODE, None),
        P(None, NODE),
        P(),
        P(),
        P(NODE, None),
        P(NODE),
        P(None, NODE, None),
    )
    out_specs = (P("section", NODE, None), P("section", NODE, None), P("section", NODE, None))
    return jax.shard_map(body, mesh=fine, in_specs=in_specs, out_specs=out_specs, check_vma=False)
```

```python
import jax
import jax.numpy as jnp
from jax import lax
from jax.experimental import pallas as pl
from jax.experimental.pallas import tpu as pltpu
from jax.sharding import Mesh, PartitionSpec as P

HEADS = 8
HALO_W = 32
STEP = 100


BETA_ONE = 0.9
BETA_TWO = 0.999
LEARN_RATE = 0.001

NODE = ("z", "x", "core")
PLANE = ("x", "core")
F32 = jnp.float32
BF16 = jnp.bfloat16
KERNEL_VMEM = 12 * 2**20


def across(index, count):
    return (index + 1) % count if index % 2 else (index - 1) % count


def swap(value):
    return lax.ppermute(value, "core", [(0, 1), (1, 0)])


def beside(value, steps):
    sections, count = lax.axis_size("section"), lax.axis_size(NODE)
    moves = [
        (section * count + index, (section + steps) * count + across(index, count))
        for section in range(sections)
        if 0 <= section + steps < sections
        for index in range(count)
    ]
    return lax.ppermute(value, ("section",) + NODE, moves)


def from_behind(value, axis, steps):
    count = lax.axis_size(axis)
    leading, last = (max(0, -steps), min(count, count - steps))
    return lax.ppermute(value, axis, [(source, source + steps) for source in range(leading, last)])


def norm_rows(values):
    return values * lax.rsqrt(jnp.mean(values * values, axis=-1, keepdims=True) + 1e-06)


def norm_pull(values, grads):
    scale = lax.rsqrt(jnp.mean(values * values, axis=-1, keepdims=True) + 1e-06)
    inner = jnp.mean(values * grads, axis=-1, keepdims=True)
    return scale * (grads - values * (inner * scale * scale))


def nt(a, b):
    return lax.dot_general(a, b, (((1,), (1,)), ((), ())), preferred_element_type=F32)


def nn(a, b):
    return lax.dot_general(a, b, (((1,), (0,)), ((), ())), preferred_element_type=F32)


def tn(a, b):
    return lax.dot_general(a, b, (((0,), (0,)), ((), ())), preferred_element_type=F32)


def spans(width, size):
    return [(start, start + size) for start in range(0, width, size)]


def rows_of(*pieces):
    return jnp.concatenate(pieces, axis=0)


def softmax_band(queries, keys, used, scale):
    scores = [nt(query, key) * scale for query, key in zip(queries, keys)]
    weights = [jnp.where(u, jnp.exp(score), 0.0) for u, score in zip(used, scores)]
    sums = [jnp.sum(weight, axis=-1, keepdims=True) for weight in weights]
    return [weight / total for weight, total in zip(weights, sums)]


def attend_kernel(side_ref, state_ref, proj_ref, mask_ref, out_ref):
    rows, width = state_ref.shape
    size = width // HEADS
    cuts = spans(width, size)
    half = rows // 2
    below = 2 - side_ref[0]
    above = 3 - below
    used = [mask_ref[...] > 0] * HEADS

    def banded(base):
        return [
            rows_of(
                proj_ref[below, half:, base + a : base + b],
                proj_ref[0, :, base + a : base + b],
                proj_ref[above, :half, base + a : base + b],
            )
            for a, b in cuts
        ]

    queries = [proj_ref[0, :, a:b] for a, b in cuts]
    probs = softmax_band(queries, banded(width), used, size ** (-0.5))
    mixed = [nn(p.astype(BF16), v) for p, v in zip(probs, banded(2 * width))]
    for (a, b), term in zip(cuts, mixed):
        out_ref[:, a:b] = (state_ref[:, a:b].astype(F32) + term).astype(BF16)


VMEM = pl.BlockSpec(memory_space=pltpu.VMEM)
SMEM = pl.BlockSpec(memory_space=pltpu.SMEM)


def attend(side, state, proj, mask):
    return pl.pallas_call(
        attend_kernel,
        out_shape=jax.ShapeDtypeStruct(state.shape, BF16),
        in_specs=[SMEM, VMEM, VMEM, VMEM],
        out_specs=VMEM,
        compiler_params=pltpu.CompilerParams(vmem_limit_bytes=KERNEL_VMEM),
        name="attend",
    )(side, state, proj, mask)


def pull_kernel(side_ref, proj_ref, mask_ref, own_ref, pair_ref, cross_ref, out_ref):
    rows, width = own_ref.shape
    size = width // HEADS
    scale = size ** (-0.5)
    cuts = spans(width, size)
    half = rows // 2
    below = 2 - side_ref[0]
    above = 3 - below

    def low_queries(a, b):
        return rows_of(proj_ref[below, half:, a:b], proj_ref[0, :half, a:b])

    def high_queries(a, b):
        return rows_of(proj_ref[0, half:, a:b], proj_ref[above, :half, a:b])

    def low_keys(a, b):
        return rows_of(proj_ref[below, :, a:b], proj_ref[0, :, a:b])

    def high_keys(a, b):
        return rows_of(proj_ref[0, :, a:b], proj_ref[above, :, a:b])

    def both(low, high, base):
        return [low(base + a, base + b) for a, b in cuts] + [
            high(base + a, base + b) for a, b in cuts
        ]

    queries = both(low_queries, high_queries, 0)
    keys = both(low_keys, high_keys, width)
    values = both(low_keys, high_keys, 2 * width)
    first = side_ref[0] == 0
    low_edge = jnp.where(first, cross_ref[...], pair_ref[...])
    high_edge = jnp.where(first, pair_ref[...], cross_ref[...])
    upstream = [rows_of(low_edge[:, a:b], own_ref[:half, a:b]) for a, b in cuts] + [
        rows_of(own_ref[half:, a:b], high_edge[:, a:b]) for a, b in cuts
    ]
    used = [mask_ref[0] > 0] * HEADS + [mask_ref[1] > 0] * HEADS
    probs = softmax_band(queries, keys, used, scale)
    grad_probs = [nt(u, v).astype(BF16).astype(F32) for u, v in zip(upstream, values)]
    inner = [jnp.sum(g * p, axis=-1, keepdims=True) for g, p in zip(grad_probs, probs)]
    grad_scores = [
        (p * (g - i) * scale).astype(BF16) for p, g, i in zip(probs, grad_probs, inner)
    ]
    rounded = [p.astype(BF16) for p in probs]
    for head, (a, b) in enumerate(cuts):
        low, high = head, HEADS + head
        out_ref[:half, a:b] = nn(grad_scores[low], keys[low])[half:].astype(BF16)
        out_ref[half:, a:b] = nn(grad_scores[high], keys[high])[:half].astype(BF16)
        for base, left, right in ((width, grad_scores, queries), (2 * width, rounded, upstream)):
            total = tn(left[low], right[low])[rows:] + tn(left[high], right[high])[:rows]
            out_ref[:, base + a : base + b] = total.astype(BF16)


def attend_pull(side, proj, masks, own, pair, cross):
    return pl.pallas_call(
        pull_kernel,
        out_shape=jax.ShapeDtypeStruct(proj.shape[1:], BF16),
        in_specs=[SMEM, VMEM, VMEM, VMEM, VMEM, VMEM],
        out_specs=VMEM,
        compiler_params=pltpu.CompilerParams(vmem_limit_bytes=KERNEL_VMEM),
        name="attend_pull",
    )(side, proj, masks, own, pair, cross)


def route(obs_rows, obs_device, obs_node, encode_weight, node_state):
    micro, nodes_dev, width = node_state.shape
    per_dev, levels = obs_rows.shape[1:]
    node_devs = lax.axis_size(NODE)
    capacity = max(2, 2 * per_dev // node_devs)
    slots = node_devs * micro * capacity
    target = obs_device[..., 0]
    named = (target[..., None] == jnp.arange(node_devs)[None, None, :]).astype(BF16)
    earlier = (jnp.arange(per_dev)[:, None] > jnp.arange(per_dev)[None, :]).astype(BF16)
    before = jnp.einsum("ij,mjd->mid", earlier, named, preferred_element_type=F32)
    ranked = jnp.sum(before * named.astype(F32), axis=-1).astype(jnp.int32)
    position = (target * micro + jnp.arange(micro)[:, None]) * capacity + ranked
    chosen = (jnp.arange(slots)[:, None] == position.reshape(1, -1)).astype(BF16)
    payload = jnp.concatenate([obs_rows, obs_node[..., None].astype(BF16)], axis=-1)
    sent = nn(chosen, payload.reshape(micro * per_dev, levels + 1)).astype(BF16)
    received = lax.all_to_all(
        sent.reshape(node_devs, micro * capacity, levels + 1),
        NODE,
        split_axis=0,
        concat_axis=0,
        tiled=True,
    ).reshape(slots, levels + 1)
    owner = received[:, levels].astype(jnp.int32)
    owner = owner + (jnp.arange(slots) // capacity % micro) * nodes_dev
    held = (jnp.arange(micro * nodes_dev)[:, None] == owner[None, :]).astype(BF16)
    summed = nn(held, received[:, :levels])
    high = lax.reduce_precision(summed, 8, 7)
    rest = summed - high
    encoded = nn(high.astype(BF16), encode_weight) + nn(rest.astype(BF16), encode_weight)
    return (node_state.astype(F32) + encoded.reshape(micro, nodes_dev, width)).astype(BF16)


def body(
    master,
    first_moment,
    second_moment,
    node_state,
    obs_rows,
    obs_device,
    obs_node,
    encode_weight,
    decode_weight,
    neighbors,
    neighbor_count,
    out_grad,
):
    sections = lax.axis_size("section")
    section = lax.axis_index("section")
    node_devs = lax.axis_size(NODE)
    micro, nodes_dev, width = node_state.shape
    total_nodes = nodes_dev * node_devs
    anchor = lax.axis_index(NODE) * nodes_dev
    plane = lax.axis_size(PLANE)
    weight_rows = master.shape[1]
    weight_full = lax.all_gather(master[0].astype(BF16), "z", axis=0, tiled=True)
    weight_full = lax.all_gather(weight_full, PLANE, axis=0, tiled=True)
    weight_full = weight_full.reshape(plane, node_devs // plane, weight_rows, 3 * width)
    weight_full = weight_full.transpose(1, 0, 2, 3).reshape(width, 3 * width)
    core = lax.axis_index("core")
    side = core.astype(jnp.int32).reshape(1)
    half = nodes_dev // 2

    def cross_edge(value, first):
        return jnp.where(first, value[..., :half, :], value[..., half:, :])

    entry = route(obs_rows, obs_device, obs_node, encode_weight, node_state)
    rim = HALO_W
    relative = (neighbors - anchor) % total_nodes
    relative = jnp.where(relative >= total_nodes - rim, relative - total_nodes, relative) + rim
    relative = relative - half * (jnp.arange(nodes_dev)[:, None] // half)
    reach = half + 2 * rim
    valid = jnp.arange(neighbors.shape[1])[None, :] < neighbor_count[:, None]
    at = (relative[..., None] == jnp.arange(reach)[None, None, :]) & valid[..., None]
    near = jnp.sum(at.astype(F32), axis=1).astype(BF16)
    head_grad = nt(out_grad.reshape(micro * nodes_dev, -1), decode_weight)
    head_grad = head_grad.astype(BF16).reshape(micro, nodes_dev, width)

    early = jnp.concatenate(
        [head_grad.reshape(-1, width), jnp.pad(near, ((0, 0), (0, width - reach)))]
    ).reshape(micro + 1, nodes_dev, width)
    from_pair = swap(cross_edge(early, core != 0))
    from_cross = beside(cross_edge(early, core == 0), 0)
    entry_cross = beside(entry, 0)
    at_stage = [section == stage for stage in range(sections)]
    entry, entry_cross, from_pair, from_cross, head_grad, first_core, side, at_stage = (
        lax.optimization_barrier(
            (entry, entry_cross, from_pair, from_cross, head_grad, core == 0, side, at_stage)
        )
    )
    head_pair, head_cross = from_pair[:micro], from_cross[:micro]
    near_pair = from_pair[micro, :, :reach]
    near_cross = from_cross[micro, :, :reach]
    near_low = jnp.where(first_core, near_cross, near_pair)
    near_high = jnp.where(first_core, near_pair, near_cross)

    def bands(upper, lower):
        room = 2 * nodes_dev - reach
        return jnp.concatenate(
            [jnp.pad(upper, ((0, 0), (0, room))), jnp.pad(lower, ((0, 0), (room, 0)))]
        ).astype(F32)

    mask = bands(near[:half], near[half:])
    masks = jnp.stack([bands(near_low, near[:half]), bands(near[half:], near_high)])

    ticks = micro + sections - 1
    incoming, incoming_cross = None, None
    saved = []
    kept_normed = [None] * micro
    for tick in range(ticks):
        state, cross = incoming, incoming_cross
        if tick == 0:
            state, cross = entry[0], entry_cross[0]
        elif tick < micro:
            state = jnp.where(at_stage[0], entry[tick], incoming)
            cross = jnp.where(at_stage[0], entry_cross[tick], incoming_cross)
        around = jnp.concatenate([state, swap(state), cross], axis=0)
        normed = norm_rows(around.astype(F32)).astype(BF16)
        proj = nn(normed, weight_full).astype(BF16).reshape(3, nodes_dev, 3 * width)
        saved.append((state, proj))
        for batch in range(micro):
            stage = tick - batch
            if stage == 0:
                kept_normed[batch] = normed[:nodes_dev]
            elif 0 < stage < sections:
                kept_normed[batch] = jnp.where(
                    at_stage[stage], normed[:nodes_dev], kept_normed[batch]
                )
        if tick + 1 < ticks:
            output = attend(side, state, proj, mask)
            incoming_cross = beside(output, 1)
            incoming = from_behind(output, "section", 1)
    returning, returning_cross = None, None
    columns = 3 * width // plane
    kept_grad = [None] * micro
    for tick in range(ticks):
        sources = {}
        for stage in range(sections):
            batch = tick - (sections - 1) + stage
            if 0 <= batch < micro:
                sources[stage] = (batch, batch + stage)
        stages = sorted(sources)
        state, proj = saved[sources[stages[0]][1]]
        for stage in stages[1:]:
            here = at_stage[stage]
            state, proj = (
                jnp.where(here, a, b) for a, b in zip(saved[sources[stage][1]], (state, proj))
            )
        last = sections - 1
        if last not in sources:
            own, pair, cross = returning, swap(cross_edge(returning, jnp.logical_not(first_core))), returning_cross
        elif tick == 0:
            own, pair, cross = head_grad[0], head_pair[0], head_cross[0]
        else:
            batch = sources[last][0]
            own = jnp.where(at_stage[last], head_grad[batch], returning)
            cross = jnp.where(at_stage[last], head_cross[batch], returning_cross)
            pair = swap(cross_edge(own, jnp.logical_not(first_core)))
        grad_qkv = attend_pull(side, proj, masks, own, pair, cross)
        for stage in stages:
            batch = sources[stage][0]
            if kept_grad[batch] is None:
                kept_grad[batch] = grad_qkv
            else:
                kept_grad[batch] = jnp.where(at_stage[stage], grad_qkv, kept_grad[batch])
        if tick + 1 < ticks:
            grad_normed = nt(grad_qkv, weight_full)
            downward = (own.astype(F32) + norm_pull(state.astype(F32), grad_normed)).astype(BF16)
            if tick + 2 == ticks:
                kept, downward = lax.optimization_barrier((jnp.stack(kept_normed), downward))
                normed_all = lax.all_gather(kept, PLANE, axis=0, tiled=False)
            returning_cross = beside(cross_edge(downward, first_core), -1)
            returning = from_behind(downward, "section", -1)
    parts = jnp.concatenate(kept_grad, axis=0).reshape(micro * nodes_dev, plane, columns)
    gathered = lax.all_to_all(
        parts.transpose(1, 0, 2), PLANE, split_axis=0, concat_axis=0, tiled=True
    )
    partial = tn(
        normed_all.reshape(plane * micro * nodes_dev, width),
        gathered.reshape(plane * micro * nodes_dev, columns),
    )
    rows = width // node_devs
    pieces = lax.all_to_all(
        partial.astype(BF16).reshape(node_devs, rows, columns),
        NODE,
        split_axis=0,
        concat_axis=0,
        tiled=True,
    )
    pieces = pieces.reshape(node_devs // plane, plane, rows, columns).astype(F32)
    gradient = jnp.sum(pieces, axis=0).transpose(1, 0, 2).reshape(1, rows, 3 * width)
    new_first = BETA_ONE * first_moment + (1.0 - BETA_ONE) * gradient
    new_second = BETA_TWO * second_moment + (1.0 - BETA_TWO) * gradient * gradient
    step_size = (
        new_first / (1.0 - BETA_ONE**STEP) / (jnp.sqrt(new_second / (1.0 - BETA_TWO**STEP)) + 1e-08)
    )
    new_weights = master - LEARN_RATE * step_size
    return (new_weights, new_first, new_second)


def solution(mesh):
    sections, node_devs = mesh.devices.shape
    fine = Mesh(mesh.devices.reshape(sections, node_devs // 8, 4, 2), ("section",) + NODE)
    in_specs = (
        P("section", NODE, None),
        P("section", NODE, None),
        P("section", NODE, None),
        P(None, NODE, None),
        P(None, NODE, None),
        P(None, NODE, None),
        P(None, NODE),
        P(),
        P(),
        P(NODE, None),
        P(NODE),
        P(None, NODE, None),
    )
    out_specs = (P("section", NODE, None), P("section", NODE, None), P("section", NODE, None))
    return jax.shard_map(body, mesh=fine, in_specs=in_specs, out_specs=out_specs, check_vma=False)
```

```python
import jax
import jax.numpy as jnp
from jax import lax
from jax.experimental import pallas as pl
from jax.experimental.pallas import tpu as pltpu
from jax.sharding import Mesh, PartitionSpec as P

HEADS = 8
HALO_W = 32
STEP = 100


BETA_ONE = 0.9
BETA_TWO = 0.999
LEARN_RATE = 0.001

NODE = ("z", "x", "core")
PLANE = ("x", "core")
F32 = jnp.float32
BF16 = jnp.bfloat16
KERNEL_VMEM = 12 * 2**20


def across(index, count):
    return (index + 1) % count if index % 2 else (index - 1) % count


def swap(value):
    return lax.ppermute(value, "core", [(0, 1), (1, 0)])


def beside(value, steps):
    sections, count = lax.axis_size("section"), lax.axis_size(NODE)
    moves = [
        (section * count + index, (section + steps) * count + across(index, count))
        for section in range(sections)
        if 0 <= section + steps < sections
        for index in range(count)
    ]
    return lax.ppermute(value, ("section",) + NODE, moves)


def from_behind(value, axis, steps):
    count = lax.axis_size(axis)
    leading, last = (max(0, -steps), min(count, count - steps))
    return lax.ppermute(value, axis, [(source, source + steps) for source in range(leading, last)])


def norm_rows(values):
    return values * lax.rsqrt(jnp.mean(values * values, axis=-1, keepdims=True) + 1e-06)


def norm_pull(values, grads):
    scale = lax.rsqrt(jnp.mean(values * values, axis=-1, keepdims=True) + 1e-06)
    inner = jnp.mean(values * grads, axis=-1, keepdims=True)
    return scale * (grads - values * (inner * scale * scale))


def nt(a, b):
    return lax.dot_general(a, b, (((1,), (1,)), ((), ())), preferred_element_type=F32)


def nn(a, b):
    return lax.dot_general(a, b, (((1,), (0,)), ((), ())), preferred_element_type=F32)


def tn(a, b):
    return lax.dot_general(a, b, (((0,), (0,)), ((), ())), preferred_element_type=F32)


def spans(width, size):
    return [(start, start + size) for start in range(0, width, size)]


def rows_of(*pieces):
    return jnp.concatenate(pieces, axis=0)


def softmax_band(queries, keys, used, scale):
    scores = [nt(query, key) * scale for query, key in zip(queries, keys)]
    weights = [jnp.where(u, jnp.exp(score), 0.0) for u, score in zip(used, scores)]
    sums = [jnp.sum(weight, axis=-1, keepdims=True) for weight in weights]
    return [weight / total for weight, total in zip(weights, sums)]


def attend_kernel(side_ref, state_ref, proj_ref, mask_ref, out_ref):
    rows, width = state_ref.shape
    size = width // HEADS
    cuts = spans(width, size)
    half = rows // 2
    below = 2 - side_ref[0]
    above = 3 - below
    used = [mask_ref[...] > 0] * HEADS

    def banded(base):
        return [
            rows_of(
                proj_ref[below, half:, base + a : base + b],
                proj_ref[0, :, base + a : base + b],
                proj_ref[above, :half, base + a : base + b],
            )
            for a, b in cuts
        ]

    queries = [proj_ref[0, :, a:b] for a, b in cuts]
    probs = softmax_band(queries, banded(width), used, size ** (-0.5))
    mixed = [nn(p.astype(BF16), v) for p, v in zip(probs, banded(2 * width))]
    for (a, b), term in zip(cuts, mixed):
        out_ref[:, a:b] = (state_ref[:, a:b].astype(F32) + term).astype(BF16)


VMEM = pl.BlockSpec(memory_space=pltpu.VMEM)
SMEM = pl.BlockSpec(memory_space=pltpu.SMEM)


def attend(side, state, proj, mask):
    return pl.pallas_call(
        attend_kernel,
        out_shape=jax.ShapeDtypeStruct(state.shape, BF16),
        in_specs=[SMEM, VMEM, VMEM, VMEM],
        out_specs=VMEM,
        compiler_params=pltpu.CompilerParams(vmem_limit_bytes=KERNEL_VMEM),
        name="attend",
    )(side, state, proj, mask)


def pull_kernel(side_ref, proj_ref, mask_ref, own_ref, edge_ref, out_ref):
    rows, width = own_ref.shape
    size = width // HEADS
    scale = size ** (-0.5)
    cuts = spans(width, size)
    half = rows // 2
    below = 2 - side_ref[0]
    above = 3 - below

    def low_queries(a, b):
        return rows_of(proj_ref[below, half:, a:b], proj_ref[0, :half, a:b])

    def high_queries(a, b):
        return rows_of(proj_ref[0, half:, a:b], proj_ref[above, :half, a:b])

    def low_keys(a, b):
        return rows_of(proj_ref[below, :, a:b], proj_ref[0, :, a:b])

    def high_keys(a, b):
        return rows_of(proj_ref[0, :, a:b], proj_ref[above, :, a:b])

    def both(low, high, base):
        return [low(base + a, base + b) for a, b in cuts] + [
            high(base + a, base + b) for a, b in cuts
        ]

    queries = both(low_queries, high_queries, 0)
    keys = both(low_keys, high_keys, width)
    values = both(low_keys, high_keys, 2 * width)
    upstream = [rows_of(edge_ref[below - 1, :, a:b], own_ref[:half, a:b]) for a, b in cuts] + [
        rows_of(own_ref[half:, a:b], edge_ref[above - 1, :, a:b]) for a, b in cuts
    ]
    used = [mask_ref[0] > 0] * HEADS + [mask_ref[1] > 0] * HEADS
    probs = softmax_band(queries, keys, used, scale)
    grad_probs = [nt(u, v).astype(BF16).astype(F32) for u, v in zip(upstream, values)]
    inner = [jnp.sum(g * p, axis=-1, keepdims=True) for g, p in zip(grad_probs, probs)]
    grad_scores = [
        (p * (g - i) * scale).astype(BF16) for p, g, i in zip(probs, grad_probs, inner)
    ]
    rounded = [p.astype(BF16) for p in probs]
    for head, (a, b) in enumerate(cuts):
        low, high = head, HEADS + head
        out_ref[:half, a:b] = nn(grad_scores[low], keys[low])[half:].astype(BF16)
        out_ref[half:, a:b] = nn(grad_scores[high], keys[high])[:half].astype(BF16)
        for base, left, right in ((width, grad_scores, queries), (2 * width, rounded, upstream)):
            total = tn(left[low], right[low])[rows:] + tn(left[high], right[high])[:rows]
            out_ref[:, base + a : base + b] = total.astype(BF16)


def attend_pull(side, proj, masks, own, edges):
    return pl.pallas_call(
        pull_kernel,
        out_shape=jax.ShapeDtypeStruct(proj.shape[1:], BF16),
        in_specs=[SMEM, VMEM, VMEM, VMEM, VMEM],
        out_specs=VMEM,
        compiler_params=pltpu.CompilerParams(vmem_limit_bytes=KERNEL_VMEM),
        name="attend_pull",
    )(side, proj, masks, own, edges)


def cycle(axis, steps):
    count = lax.axis_size(axis)
    return [(i, (i + steps) % count) for i in range(count)]


def around_ring(value, axis):
    count = lax.axis_size(axis)
    pieces, ahead, back = {0: value}, value, value
    for step in range(1, count // 2 + 1):
        ahead = lax.ppermute(ahead, axis, cycle(axis, 1))
        pieces[step] = ahead
        if step < count - step:
            back = lax.ppermute(back, axis, cycle(axis, -1))
            pieces[count - step] = back
    return [pieces[step] for step in range(count)]


def place_kernel(place_ref, *refs):
    pieces, out_ref, sems = refs[:-2], refs[-2], refs[-1]
    zs, xs = 8, 4
    rows = out_ref.shape[0] // (2 * zs * xs)
    z, x, core = place_ref[0], place_ref[1], place_ref[2]
    copies = []
    for step in range(zs):
        for hop in range(xs):
            for side in range(2):
                index = (((z + zs - step) % zs) * xs + (x + xs - hop) % xs) * 2 + (core + side) % 2
                to = pl.multiple_of(index * rows, rows)
                copies.append(
                    pltpu.make_async_copy(
                        pieces[side * zs + step].at[pl.ds(hop * rows, rows)],
                        out_ref.at[pl.ds(to, rows)],
                        sems.at[len(copies)],
                    )
                )
    for copy in copies:
        copy.start()
    for copy in copies:
        copy.wait()


def gather_weights(shard):
    rows, columns = shard.shape
    hops = [shard] + [lax.ppermute(shard, "x", cycle("x", hop)) for hop in range(1, 4)]
    own = around_ring(jnp.concatenate(hops, axis=0), "z")
    other = [swap(piece) for piece in own]
    total = 2 * len(own) * len(hops)
    place = jnp.stack([lax.axis_index(axis) for axis in NODE]).astype(jnp.int32)
    return pl.pallas_call(
        place_kernel,
        out_shape=jax.ShapeDtypeStruct((total * rows, columns), BF16),
        in_specs=[SMEM] + [pl.BlockSpec(memory_space=pl.ANY)] * (2 * len(own)),
        out_specs=VMEM,
        scratch_shapes=[pltpu.SemaphoreType.DMA((total,))],
        compiler_params=pltpu.CompilerParams(vmem_limit_bytes=KERNEL_VMEM),
        name="place_weights",
    )(place, *own, *other)


def route(obs_rows, obs_device, obs_node, encode_weight, node_state):
    micro, nodes_dev, width = node_state.shape
    per_dev, levels = obs_rows.shape[1:]
    node_devs = lax.axis_size(NODE)
    capacity = max(2, 2 * per_dev // node_devs)
    slots = node_devs * micro * capacity
    target = obs_device[..., 0]
    named = (target[..., None] == jnp.arange(node_devs)[None, None, :]).astype(BF16)
    earlier = (jnp.arange(per_dev)[:, None] > jnp.arange(per_dev)[None, :]).astype(BF16)
    before = jnp.einsum("ij,mjd->mid", earlier, named, preferred_element_type=F32)
    ranked = jnp.sum(before * named.astype(F32), axis=-1).astype(jnp.int32)
    position = (target * micro + jnp.arange(micro)[:, None]) * capacity + ranked
    chosen = (jnp.arange(slots)[:, None] == position.reshape(1, -1)).astype(BF16)
    payload = jnp.concatenate([obs_rows, obs_node[..., None].astype(BF16)], axis=-1)
    sent = nn(chosen, payload.reshape(micro * per_dev, levels + 1)).astype(BF16)
    received = lax.all_to_all(
        sent.reshape(node_devs, micro * capacity, levels + 1),
        NODE,
        split_axis=0,
        concat_axis=0,
        tiled=True,
    ).reshape(slots, levels + 1)
    owner = received[:, levels].astype(jnp.int32)
    owner = owner + (jnp.arange(slots) // capacity % micro) * nodes_dev
    held = (jnp.arange(micro * nodes_dev)[:, None] == owner[None, :]).astype(BF16)
    summed = nn(held, received[:, :levels])
    high = lax.reduce_precision(summed, 8, 7)
    rest = summed - high
    encoded = nn(high.astype(BF16), encode_weight) + nn(rest.astype(BF16), encode_weight)
    return (node_state.astype(F32) + encoded.reshape(micro, nodes_dev, width)).astype(BF16)


def body(
    master,
    first_moment,
    second_moment,
    node_state,
    obs_rows,
    obs_device,
    obs_node,
    encode_weight,
    decode_weight,
    neighbors,
    neighbor_count,
    out_grad,
):
    sections = lax.axis_size("section")
    section = lax.axis_index("section")
    node_devs = lax.axis_size(NODE)
    micro, nodes_dev, width = node_state.shape
    total_nodes = nodes_dev * node_devs
    anchor = lax.axis_index(NODE) * nodes_dev
    plane = lax.axis_size(PLANE)
    weight_full = gather_weights(master[0].astype(BF16))
    core = lax.axis_index("core")
    side = core.astype(jnp.int32).reshape(1)
    half = nodes_dev // 2

    def pair_edge(value, first):
        return jnp.where(first, value[..., half:, :], value[..., :half, :])

    def cross_edge(value, first):
        return jnp.where(first, value[..., :half, :], value[..., half:, :])

    entry = route(obs_rows, obs_device, obs_node, encode_weight, node_state)
    rim = HALO_W
    relative = (neighbors - anchor) % total_nodes
    relative = jnp.where(relative >= total_nodes - rim, relative - total_nodes, relative) + rim
    relative = relative - half * (jnp.arange(nodes_dev)[:, None] // half)
    reach = half + 2 * rim
    valid = jnp.arange(neighbors.shape[1])[None, :] < neighbor_count[:, None]
    at = (relative[..., None] == jnp.arange(reach)[None, None, :]) & valid[..., None]
    near = jnp.sum(at.astype(F32), axis=1).astype(BF16)
    head_grad = nt(out_grad.reshape(micro * nodes_dev, -1), decode_weight)
    head_grad = head_grad.astype(BF16).reshape(micro, nodes_dev, width)

    def packed(edge):
        return jnp.concatenate(
            [
                edge(head_grad, core == 0).reshape(-1, width),
                jnp.pad(edge(near, core == 0), ((0, 0), (0, width - reach))),
            ]
        )

    from_pair = swap(packed(pair_edge))
    from_cross = beside(jnp.concatenate([packed(cross_edge), entry.reshape(-1, width)]), 0)
    at_stage = [section == stage for stage in range(sections)]
    entry, from_pair, from_cross, head_grad, first_core, side, at_stage = lax.optimization_barrier(
        (entry, from_pair, from_cross, head_grad, core == 0, side, at_stage)
    )
    heads = micro * half
    head_pair = from_pair[:heads].reshape(micro, half, width)
    head_cross = from_cross[:heads].reshape(micro, half, width)
    near_pair = from_pair[heads : heads + half, :reach]
    near_cross = from_cross[heads : heads + half, :reach]
    entry_cross = from_cross[heads + half :].reshape(micro, nodes_dev, width)
    near_low = jnp.where(first_core, near_cross, near_pair)
    near_high = jnp.where(first_core, near_pair, near_cross)

    def bands(upper, lower):
        room = 2 * nodes_dev - reach
        return jnp.concatenate(
            [jnp.pad(upper, ((0, 0), (0, room))), jnp.pad(lower, ((0, 0), (room, 0)))]
        ).astype(F32)

    mask = bands(near[:half], near[half:])
    masks = jnp.stack([bands(near_low, near[:half]), bands(near[half:], near_high)])

    ticks = micro + sections - 1
    incoming, incoming_cross = None, None
    saved = []
    kept_normed = [None] * micro
    for tick in range(ticks):
        state, cross = incoming, incoming_cross
        if tick == 0:
            state, cross = entry[0], entry_cross[0]
        elif tick < micro:
            state = jnp.where(at_stage[0], entry[tick], incoming)
            cross = jnp.where(at_stage[0], entry_cross[tick], incoming_cross)
        around = jnp.concatenate([state, swap(state), cross], axis=0)
        normed = norm_rows(around.astype(F32)).astype(BF16)
        proj = nn(normed, weight_full).astype(BF16).reshape(3, nodes_dev, 3 * width)
        saved.append((state, proj))
        for batch in range(micro):
            stage = tick - batch
            if stage == 0:
                kept_normed[batch] = normed[:nodes_dev]
            elif 0 < stage < sections:
                kept_normed[batch] = jnp.where(
                    at_stage[stage], normed[:nodes_dev], kept_normed[batch]
                )
        if tick + 1 < ticks:
            output = attend(side, state, proj, mask)
            incoming_cross = beside(output, 1)
            incoming = from_behind(output, "section", 1)
    kept = jnp.concatenate(kept_normed, axis=0)
    x = lax.axis_index("x")
    returning, returning_cross = None, None
    columns = 3 * width // plane
    kept_grad = [None] * micro
    for tick in range(ticks):
        sources = {}
        for stage in range(sections):
            batch = tick - (sections - 1) + stage
            if 0 <= batch < micro:
                sources[stage] = (batch, batch + stage)
        stages = sorted(sources)
        state, proj = saved[sources[stages[0]][1]]
        for stage in stages[1:]:
            here = at_stage[stage]
            state, proj = (
                jnp.where(here, a, b) for a, b in zip(saved[sources[stage][1]], (state, proj))
            )
        last = sections - 1
        if last not in sources:
            own, pair, cross = returning, swap(pair_edge(returning, first_core)), returning_cross
        elif tick == 0:
            own, pair, cross = head_grad[0], head_pair[0], head_cross[0]
        else:
            batch = sources[last][0]
            own = jnp.where(at_stage[last], head_grad[batch], returning)
            cross = jnp.where(at_stage[last], head_cross[batch], returning_cross)
            pair = swap(pair_edge(own, first_core))
        grad_qkv = attend_pull(side, proj, masks, own, jnp.stack([pair, cross]))
        for stage in stages:
            batch = sources[stage][0]
            if kept_grad[batch] is None:
                kept_grad[batch] = grad_qkv
            else:
                kept_grad[batch] = jnp.where(at_stage[stage], grad_qkv, kept_grad[batch])
        if tick + 1 < ticks:
            grad_normed = nt(grad_qkv, weight_full)
            downward = (own.astype(F32) + norm_pull(state.astype(F32), grad_normed)).astype(BF16)
            if tick == ticks - 4:
                kept, downward = lax.optimization_barrier((kept, downward))
                hops = [kept] + [lax.ppermute(kept, "x", cycle("x", hop)) for hop in range(1, 4)]
            if tick == ticks - 3:
                hops, downward = lax.optimization_barrier((hops, downward))
                hops = jnp.stack(hops)
                mine = jnp.stack(
                    [
                        lax.dynamic_index_in_dim(hops, (x + 4 - source) % 4, 0, False)
                        for source in range(4)
                    ]
                )
                theirs = swap(mine)
            if tick == ticks - 2:
                theirs, downward = lax.optimization_barrier((theirs, downward))
                normed_all = jnp.stack(
                    [jnp.where(first_core, mine, theirs), jnp.where(first_core, theirs, mine)],
                    axis=1,
                )
            returning_cross = beside(cross_edge(downward, first_core), -1)
            returning = from_behind(downward, "section", -1)
    parts = jnp.concatenate(kept_grad, axis=0).reshape(micro * nodes_dev, plane, columns)
    gathered = lax.all_to_all(
        parts.transpose(1, 0, 2), PLANE, split_axis=0, concat_axis=0, tiled=True
    )
    partial = tn(
        normed_all.reshape(plane * micro * nodes_dev, width),
        gathered.reshape(plane * micro * nodes_dev, columns),
    )
    rows = width // node_devs
    pieces = lax.all_to_all(
        partial.astype(BF16).reshape(node_devs, rows, columns),
        NODE,
        split_axis=0,
        concat_axis=0,
        tiled=True,
    )
    pieces = pieces.reshape(node_devs // plane, plane, rows, columns).astype(F32)
    gradient = jnp.sum(pieces, axis=0).transpose(1, 0, 2).reshape(1, rows, 3 * width)
    new_first = BETA_ONE * first_moment + (1.0 - BETA_ONE) * gradient
    new_second = BETA_TWO * second_moment + (1.0 - BETA_TWO) * gradient * gradient
    step_size = (
        new_first / (1.0 - BETA_ONE**STEP) / (jnp.sqrt(new_second / (1.0 - BETA_TWO**STEP)) + 1e-08)
    )
    new_weights = master - LEARN_RATE * step_size
    return (new_weights, new_first, new_second)


def solution(mesh):
    sections, node_devs = mesh.devices.shape
    fine = Mesh(mesh.devices.reshape(sections, node_devs // 8, 4, 2), ("section",) + NODE)
    in_specs = (
        P("section", NODE, None),
        P("section", NODE, None),
        P("section", NODE, None),
        P(None, NODE, None),
        P(None, NODE, None),
        P(None, NODE, None),
        P(None, NODE),
        P(),
        P(),
        P(NODE, None),
        P(NODE),
        P(None, NODE, None),
    )
    out_specs = (P("section", NODE, None), P("section", NODE, None), P("section", NODE, None))
    return jax.shard_map(body, mesh=fine, in_specs=in_specs, out_specs=out_specs, check_vma=False)
```

```python
import jax
import jax.numpy as jnp
from jax import lax
from jax.experimental import pallas as pl
from jax.experimental.pallas import tpu as pltpu
from jax.sharding import Mesh, PartitionSpec as P

HEADS = 8
HALO_W = 32
STEP = 100


BETA_ONE = 0.9
BETA_TWO = 0.999
LEARN_RATE = 0.001

NODE = ("z", "x", "core")
PLANE = ("x", "core")
F32 = jnp.float32
BF16 = jnp.bfloat16
KERNEL_VMEM = 12 * 2**20


def across(index, count):
    return (index + 1) % count if index % 2 else (index - 1) % count


def swap(value):
    return lax.ppermute(value, "core", [(0, 1), (1, 0)])


def beside(value, steps):
    sections, count = lax.axis_size("section"), lax.axis_size(NODE)
    moves = [
        (section * count + index, (section + steps) * count + across(index, count))
        for section in range(sections)
        if 0 <= section + steps < sections
        for index in range(count)
    ]
    return lax.ppermute(value, ("section",) + NODE, moves)


def from_behind(value, axis, steps):
    count = lax.axis_size(axis)
    leading, last = (max(0, -steps), min(count, count - steps))
    return lax.ppermute(value, axis, [(source, source + steps) for source in range(leading, last)])


def norm_rows(values):
    return values * lax.rsqrt(jnp.mean(values * values, axis=-1, keepdims=True) + 1e-06)


def norm_pull(values, grads):
    scale = lax.rsqrt(jnp.mean(values * values, axis=-1, keepdims=True) + 1e-06)
    inner = jnp.mean(values * grads, axis=-1, keepdims=True)
    return scale * (grads - values * (inner * scale * scale))


def nt(a, b):
    return lax.dot_general(a, b, (((1,), (1,)), ((), ())), preferred_element_type=F32)


def nn(a, b):
    return lax.dot_general(a, b, (((1,), (0,)), ((), ())), preferred_element_type=F32)


def tn(a, b):
    return lax.dot_general(a, b, (((0,), (0,)), ((), ())), preferred_element_type=F32)


def spans(width, size):
    return [(start, start + size) for start in range(0, width, size)]


def rows_of(*pieces):
    return jnp.concatenate(pieces, axis=0)


def softmax_band(queries, keys, used, scale):
    scores = [nt(query, key) * scale for query, key in zip(queries, keys)]
    weights = [jnp.where(u, jnp.exp(score), 0.0) for u, score in zip(used, scores)]
    sums = [jnp.sum(weight, axis=-1, keepdims=True) for weight in weights]
    return [weight / total for weight, total in zip(weights, sums)]


def attend_kernel(side_ref, state_ref, proj_ref, mask_ref, out_ref):
    rows, width = state_ref.shape
    size = width // HEADS
    cuts = spans(width, size)
    half = rows // 2
    below = 2 - side_ref[0]
    above = 3 - below
    used = [mask_ref[...] > 0] * HEADS

    def banded(base):
        return [
            rows_of(
                proj_ref[below, half:, base + a : base + b],
                proj_ref[0, :, base + a : base + b],
                proj_ref[above, :half, base + a : base + b],
            )
            for a, b in cuts
        ]

    queries = [proj_ref[0, :, a:b] for a, b in cuts]
    probs = softmax_band(queries, banded(width), used, size ** (-0.5))
    mixed = [nn(p.astype(BF16), v) for p, v in zip(probs, banded(2 * width))]
    for (a, b), term in zip(cuts, mixed):
        out_ref[:, a:b] = (state_ref[:, a:b].astype(F32) + term).astype(BF16)


VMEM = pl.BlockSpec(memory_space=pltpu.VMEM)
SMEM = pl.BlockSpec(memory_space=pltpu.SMEM)


def attend(side, state, proj, mask):
    return pl.pallas_call(
        attend_kernel,
        out_shape=jax.ShapeDtypeStruct(state.shape, BF16),
        in_specs=[SMEM, VMEM, VMEM, VMEM],
        out_specs=VMEM,
        compiler_params=pltpu.CompilerParams(vmem_limit_bytes=KERNEL_VMEM),
        name="attend",
    )(side, state, proj, mask)


def pull_kernel(side_ref, proj_ref, mask_ref, own_ref, edge_ref, out_ref):
    rows, width = own_ref.shape
    size = width // HEADS
    scale = size ** (-0.5)
    cuts = spans(width, size)
    half = rows // 2
    below = 2 - side_ref[0]
    above = 3 - below

    def low_queries(a, b):
        return rows_of(proj_ref[below, half:, a:b], proj_ref[0, :half, a:b])

    def high_queries(a, b):
        return rows_of(proj_ref[0, half:, a:b], proj_ref[above, :half, a:b])

    def low_keys(a, b):
        return rows_of(proj_ref[below, :, a:b], proj_ref[0, :, a:b])

    def high_keys(a, b):
        return rows_of(proj_ref[0, :, a:b], proj_ref[above, :, a:b])

    def both(low, high, base):
        return [low(base + a, base + b) for a, b in cuts] + [
            high(base + a, base + b) for a, b in cuts
        ]

    queries = both(low_queries, high_queries, 0)
    keys = both(low_keys, high_keys, width)
    values = both(low_keys, high_keys, 2 * width)
    upstream = [rows_of(edge_ref[below - 1, :, a:b], own_ref[:half, a:b]) for a, b in cuts] + [
        rows_of(own_ref[half:, a:b], edge_ref[above - 1, :, a:b]) for a, b in cuts
    ]
    used = [mask_ref[0] > 0] * HEADS + [mask_ref[1] > 0] * HEADS
    probs = softmax_band(queries, keys, used, scale)
    grad_probs = [nt(u, v).astype(BF16).astype(F32) for u, v in zip(upstream, values)]
    inner = [jnp.sum(g * p, axis=-1, keepdims=True) for g, p in zip(grad_probs, probs)]
    grad_scores = [
        (p * (g - i) * scale).astype(BF16) for p, g, i in zip(probs, grad_probs, inner)
    ]
    rounded = [p.astype(BF16) for p in probs]
    for head, (a, b) in enumerate(cuts):
        low, high = head, HEADS + head
        out_ref[:half, a:b] = nn(grad_scores[low], keys[low])[half:].astype(BF16)
        out_ref[half:, a:b] = nn(grad_scores[high], keys[high])[:half].astype(BF16)
        for base, left, right in ((width, grad_scores, queries), (2 * width, rounded, upstream)):
            total = tn(left[low], right[low])[rows:] + tn(left[high], right[high])[:rows]
            out_ref[:, base + a : base + b] = total.astype(BF16)


def attend_pull(side, proj, masks, own, edges):
    return pl.pallas_call(
        pull_kernel,
        out_shape=jax.ShapeDtypeStruct(proj.shape[1:], BF16),
        in_specs=[SMEM, VMEM, VMEM, VMEM, VMEM],
        out_specs=VMEM,
        compiler_params=pltpu.CompilerParams(vmem_limit_bytes=KERNEL_VMEM),
        name="attend_pull",
    )(side, proj, masks, own, edges)


def cycle(axis, steps):
    count = lax.axis_size(axis)
    return [(i, (i + steps) % count) for i in range(count)]


def place_kernel(place_ref, *refs):
    pieces, out_ref = refs[:-1], refs[-1]
    zs, xs = 8, 4
    rows = out_ref.shape[0] // (2 * zs * xs)
    z, x, core = place_ref[0], place_ref[1], place_ref[2]
    for step in range(zs):
        for hop in range(xs):
            for side in range(2):
                index = (((z + zs - step) % zs) * xs + (x + xs - hop) % xs) * 2 + (core + side) % 2
                to = pl.multiple_of(index * rows, rows)
                out_ref[pl.ds(to, rows), :] = pieces[side * zs + step][
                    hop * rows : (hop + 1) * rows, :
                ]


def gather_column(shard):
    hops = [shard] + [lax.ppermute(shard, "x", cycle("x", hop)) for hop in range(1, 4)]
    return jnp.concatenate(hops, axis=0)


def ring_step(ahead, back):
    return lax.ppermute(ahead, "z", cycle("z", 1)), lax.ppermute(back, "z", cycle("z", -1))


def place_weights(own):
    other = [swap(piece) for piece in own]
    place = jnp.stack([lax.axis_index(axis) for axis in NODE]).astype(jnp.int32)
    return pl.pallas_call(
        place_kernel,
        out_shape=jax.ShapeDtypeStruct((2 * len(own) * own[0].shape[0], own[0].shape[1]), BF16),
        in_specs=[SMEM] + [VMEM] * (2 * len(own)),
        out_specs=VMEM,
        compiler_params=pltpu.CompilerParams(vmem_limit_bytes=2 * KERNEL_VMEM),
        name="place_weights",
    )(place, *own, *other)


def route_out(obs_rows, obs_device, obs_node, micro):
    per_dev, levels = obs_rows.shape[1:]
    node_devs = lax.axis_size(NODE)
    capacity = max(2, 2 * per_dev // node_devs)
    slots = node_devs * micro * capacity
    target = obs_device[..., 0]
    named = (target[..., None] == jnp.arange(node_devs)[None, None, :]).astype(BF16)
    earlier = (jnp.arange(per_dev)[:, None] > jnp.arange(per_dev)[None, :]).astype(BF16)
    before = jnp.einsum("ij,mjd->mid", earlier, named, preferred_element_type=F32)
    ranked = jnp.sum(before * named.astype(F32), axis=-1).astype(jnp.int32)
    position = (target * micro + jnp.arange(micro)[:, None]) * capacity + ranked
    chosen = (jnp.arange(slots)[:, None] == position.reshape(1, -1)).astype(BF16)
    payload = jnp.concatenate([obs_rows, obs_node[..., None].astype(BF16)], axis=-1)
    sent = nn(chosen, payload.reshape(micro * per_dev, levels + 1)).astype(BF16)
    return sent.reshape(node_devs, micro * capacity, levels + 1)


def route_in(received, encode_weight, node_state):
    micro, nodes_dev, width = node_state.shape
    node_devs, held_slots, columns = received.shape
    levels, slots, capacity = columns - 1, node_devs * held_slots, held_slots // micro
    received = received.reshape(slots, columns)
    owner = received[:, levels].astype(jnp.int32)
    owner = owner + (jnp.arange(slots) // capacity % micro) * nodes_dev
    held = (jnp.arange(micro * nodes_dev)[:, None] == owner[None, :]).astype(BF16)
    summed = nn(held, received[:, :levels])
    high = lax.reduce_precision(summed, 8, 7)
    rest = summed - high
    encoded = nn(high.astype(BF16), encode_weight) + nn(rest.astype(BF16), encode_weight)
    return (node_state.astype(F32) + encoded.reshape(micro, nodes_dev, width)).astype(BF16)


def body(
    master,
    first_moment,
    second_moment,
    node_state,
    obs_rows,
    obs_device,
    obs_node,
    encode_weight,
    decode_weight,
    neighbors,
    neighbor_count,
    out_grad,
):
    sections = lax.axis_size("section")
    section = lax.axis_index("section")
    node_devs = lax.axis_size(NODE)
    micro, nodes_dev, width = node_state.shape
    total_nodes = nodes_dev * node_devs
    anchor = lax.axis_index(NODE) * nodes_dev
    plane = lax.axis_size(PLANE)
    sent = route_out(obs_rows, obs_device, obs_node, micro)
    column = gather_column(master[0].astype(BF16))
    sent, column = lax.optimization_barrier((sent, column))
    received = lax.all_to_all(sent, NODE, split_axis=0, concat_axis=0, tiled=True)
    first = ring_step(column, column)
    second = ring_step(*first)
    received, second = lax.optimization_barrier((received, second))
    core = lax.axis_index("core")
    side = core.astype(jnp.int32).reshape(1)
    half = nodes_dev // 2

    def pair_edge(value, first):
        return jnp.where(first, value[..., half:, :], value[..., :half, :])

    def cross_edge(value, first):
        return jnp.where(first, value[..., :half, :], value[..., half:, :])

    entry = route_in(received, encode_weight, node_state)
    rim = HALO_W
    relative = (neighbors - anchor) % total_nodes
    relative = jnp.where(relative >= total_nodes - rim, relative - total_nodes, relative) + rim
    relative = relative - half * (jnp.arange(nodes_dev)[:, None] // half)
    reach = half + 2 * rim
    valid = jnp.arange(neighbors.shape[1])[None, :] < neighbor_count[:, None]
    at = (relative[..., None] == jnp.arange(reach)[None, None, :]) & valid[..., None]
    near = jnp.sum(at.astype(F32), axis=1).astype(BF16)
    head_grad = nt(out_grad.reshape(micro * nodes_dev, -1), decode_weight)
    head_grad = head_grad.astype(BF16).reshape(micro, nodes_dev, width)

    def packed(edge):
        return jnp.concatenate(
            [
                edge(head_grad, core == 0).reshape(-1, width),
                jnp.pad(edge(near, core == 0), ((0, 0), (0, width - reach))),
            ]
        )

    from_pair = swap(packed(pair_edge))
    from_cross = beside(jnp.concatenate([packed(cross_edge), entry.reshape(-1, width)]), 0)
    third = ring_step(*second)
    from_cross, third = lax.optimization_barrier((from_cross, third))
    fourth = lax.ppermute(third[0], "z", cycle("z", 1))
    pieces = [column, first[0], second[0], third[0], fourth, third[1], second[1], first[1]]
    x = lax.axis_index("x")
    turns = [((x + 4 - source) % 4).astype(jnp.uint32) for source in range(4)]
    at_stage = [section == stage for stage in range(sections)]
    entry, from_pair, from_cross, head_grad, first_core, side, at_stage, turns = (
        lax.optimization_barrier(
            (entry, from_pair, from_cross, head_grad, core == 0, side, at_stage, turns)
        )
    )
    weight_full = place_weights(pieces)
    heads = micro * half
    head_pair = from_pair[:heads].reshape(micro, half, width)
    head_cross = from_cross[:heads].reshape(micro, half, width)
    near_pair = from_pair[heads : heads + half, :reach]
    near_cross = from_cross[heads : heads + half, :reach]
    entry_cross = from_cross[heads + half :].reshape(micro, nodes_dev, width)
    near_low = jnp.where(first_core, near_cross, near_pair)
    near_high = jnp.where(first_core, near_pair, near_cross)

    def bands(upper, lower):
        room = 2 * nodes_dev - reach
        return jnp.concatenate(
            [jnp.pad(upper, ((0, 0), (0, room))), jnp.pad(lower, ((0, 0), (room, 0)))]
        ).astype(F32)

    mask = bands(near[:half], near[half:])
    masks = jnp.stack([bands(near_low, near[:half]), bands(near[half:], near_high)])

    ticks = micro + sections - 1
    incoming, incoming_cross = None, None
    saved = []
    kept_normed = [None] * micro
    for tick in range(ticks):
        state, cross = incoming, incoming_cross
        if tick == 0:
            state, cross = entry[0], entry_cross[0]
        elif tick < micro:
            state = jnp.where(at_stage[0], entry[tick], incoming)
            cross = jnp.where(at_stage[0], entry_cross[tick], incoming_cross)
        around = jnp.concatenate([state, swap(state), cross], axis=0)
        normed = norm_rows(around.astype(F32)).astype(BF16)
        proj = nn(normed, weight_full).astype(BF16).reshape(3, nodes_dev, 3 * width)
        saved.append((state, proj))
        for batch in range(micro):
            stage = tick - batch
            if stage == 0:
                kept_normed[batch] = normed[:nodes_dev]
            elif 0 < stage < sections:
                kept_normed[batch] = jnp.where(
                    at_stage[stage], normed[:nodes_dev], kept_normed[batch]
                )
        if tick + 1 < ticks:
            output = attend(side, state, proj, mask)
            incoming_cross = beside(output, 1)
            incoming = from_behind(output, "section", 1)
    kept = jnp.concatenate(kept_normed, axis=0)
    hops = [kept] + [lax.ppermute(kept, "x", cycle("x", hop)) for hop in range(1, 4)]
    hops = jnp.stack(hops)
    mine = jnp.stack([lax.dynamic_index_in_dim(hops, turn, 0, False) for turn in turns])
    theirs = swap(mine)
    normed_all = jnp.stack(
        [jnp.where(first_core, mine, theirs), jnp.where(first_core, theirs, mine)], axis=1
    )
    returning, returning_cross = None, None
    columns = 3 * width // plane
    kept_grad = [None] * micro
    for tick in range(ticks):
        sources = {}
        for stage in range(sections):
            batch = tick - (sections - 1) + stage
            if 0 <= batch < micro:
                sources[stage] = (batch, batch + stage)
        stages = sorted(sources)
        state, proj = saved[sources[stages[0]][1]]
        for stage in stages[1:]:
            here = at_stage[stage]
            state, proj = (
                jnp.where(here, a, b) for a, b in zip(saved[sources[stage][1]], (state, proj))
            )
        last = sections - 1
        if last not in sources:
            own, pair, cross = returning, swap(pair_edge(returning, first_core)), returning_cross
        elif tick == 0:
            own, pair, cross = head_grad[0], head_pair[0], head_cross[0]
        else:
            batch = sources[last][0]
            own = jnp.where(at_stage[last], head_grad[batch], returning)
            cross = jnp.where(at_stage[last], head_cross[batch], returning_cross)
            pair = swap(pair_edge(own, first_core))
        grad_qkv = attend_pull(side, proj, masks, own, jnp.stack([pair, cross]))
        for stage in stages:
            batch = sources[stage][0]
            if kept_grad[batch] is None:
                kept_grad[batch] = grad_qkv
            else:
                kept_grad[batch] = jnp.where(at_stage[stage], grad_qkv, kept_grad[batch])
        if tick + 1 < ticks:
            grad_normed = nt(grad_qkv, weight_full)
            downward = (own.astype(F32) + norm_pull(state.astype(F32), grad_normed)).astype(BF16)
            returning_cross = beside(cross_edge(downward, first_core), -1)
            returning = from_behind(downward, "section", -1)
    parts = jnp.concatenate(kept_grad, axis=0).reshape(micro * nodes_dev, plane, columns)
    gathered = lax.all_to_all(
        parts.transpose(1, 0, 2), PLANE, split_axis=0, concat_axis=0, tiled=True
    )
    partial = tn(
        normed_all.reshape(plane * micro * nodes_dev, width),
        gathered.reshape(plane * micro * nodes_dev, columns),
    )
    rows = width // node_devs
    pieces = lax.all_to_all(
        partial.astype(BF16).reshape(node_devs, rows, columns),
        NODE,
        split_axis=0,
        concat_axis=0,
        tiled=True,
    )
    pieces = pieces.reshape(node_devs // plane, plane, rows, columns).astype(F32)
    gradient = jnp.sum(pieces, axis=0).transpose(1, 0, 2).reshape(1, rows, 3 * width)
    new_first = BETA_ONE * first_moment + (1.0 - BETA_ONE) * gradient
    new_second = BETA_TWO * second_moment + (1.0 - BETA_TWO) * gradient * gradient
    step_size = (
        new_first / (1.0 - BETA_ONE**STEP) / (jnp.sqrt(new_second / (1.0 - BETA_TWO**STEP)) + 1e-08)
    )
    new_weights = master - LEARN_RATE * step_size
    return (new_weights, new_first, new_second)


def solution(mesh):
    sections, node_devs = mesh.devices.shape
    fine = Mesh(mesh.devices.reshape(sections, node_devs // 8, 4, 2), ("section",) + NODE)
    in_specs = (
        P("section", NODE, None),
        P("section", NODE, None),
        P("section", NODE, None),
        P(None, NODE, None),
        P(None, NODE, None),
        P(None, NODE, None),
        P(None, NODE),
        P(),
        P(),
        P(NODE, None),
        P(NODE),
        P(None, NODE, None),
    )
    out_specs = (P("section", NODE, None), P("section", NODE, None), P("section", NODE, None))
    return jax.shard_map(body, mesh=fine, in_specs=in_specs, out_specs=out_specs, check_vma=False)
```

```python
import jax
import jax.numpy as jnp
from jax import lax
from jax.experimental import pallas as pl
from jax.experimental.pallas import tpu as pltpu
from jax.sharding import Mesh, PartitionSpec as P

HEADS = 8
HALO_W = 32
STEP = 100


BETA_ONE = 0.9
BETA_TWO = 0.999
LEARN_RATE = 0.001

NODE = ("z", "x", "core")
PLANE = ("x", "core")
F32 = jnp.float32
BF16 = jnp.bfloat16
KERNEL_VMEM = 12 * 2**20


def across(index, count):
    return (index + 1) % count if index % 2 else (index - 1) % count


def swap(value):
    return lax.ppermute(value, "core", [(0, 1), (1, 0)])


def beside(value, steps):
    sections, count = lax.axis_size("section"), lax.axis_size(NODE)
    moves = [
        (section * count + index, (section + steps) * count + across(index, count))
        for section in range(sections)
        if 0 <= section + steps < sections
        for index in range(count)
    ]
    return lax.ppermute(value, ("section",) + NODE, moves)


def from_behind(value, axis, steps):
    count = lax.axis_size(axis)
    leading, last = (max(0, -steps), min(count, count - steps))
    return lax.ppermute(value, axis, [(source, source + steps) for source in range(leading, last)])


def norm_rows(values):
    return values * lax.rsqrt(jnp.mean(values * values, axis=-1, keepdims=True) + 1e-06)


def norm_pull(values, grads):
    scale = lax.rsqrt(jnp.mean(values * values, axis=-1, keepdims=True) + 1e-06)
    inner = jnp.mean(values * grads, axis=-1, keepdims=True)
    return scale * (grads - values * (inner * scale * scale))


def nt(a, b):
    return lax.dot_general(a, b, (((1,), (1,)), ((), ())), preferred_element_type=F32)


def nn(a, b):
    return lax.dot_general(a, b, (((1,), (0,)), ((), ())), preferred_element_type=F32)


def tn(a, b):
    return lax.dot_general(a, b, (((0,), (0,)), ((), ())), preferred_element_type=F32)


def spans(width, size):
    return [(start, start + size) for start in range(0, width, size)]


def rows_of(*pieces):
    return jnp.concatenate(pieces, axis=0)


def softmax_band(queries, keys, used, scale):
    scores = [nt(query, key) * scale for query, key in zip(queries, keys)]
    weights = [jnp.where(u, jnp.exp(score), 0.0) for u, score in zip(used, scores)]
    sums = [jnp.sum(weight, axis=-1, keepdims=True) for weight in weights]
    return [weight / total for weight, total in zip(weights, sums)]


def attend_kernel(side_ref, state_ref, proj_ref, mask_ref, out_ref):
    rows, width = state_ref.shape
    size = width // HEADS
    cuts = spans(width, size)
    half = rows // 2
    below = 2 - side_ref[0]
    above = 3 - below
    used = [mask_ref[...] > 0] * HEADS

    def banded(base):
        return [
            rows_of(
                proj_ref[below, half:, base + a : base + b],
                proj_ref[0, :, base + a : base + b],
                proj_ref[above, :half, base + a : base + b],
            )
            for a, b in cuts
        ]

    queries = [proj_ref[0, :, a:b] for a, b in cuts]
    probs = softmax_band(queries, banded(width), used, size ** (-0.5))
    mixed = [nn(p.astype(BF16), v) for p, v in zip(probs, banded(2 * width))]
    for (a, b), term in zip(cuts, mixed):
        out_ref[:, a:b] = (state_ref[:, a:b].astype(F32) + term).astype(BF16)


VMEM = pl.BlockSpec(memory_space=pltpu.VMEM)
SMEM = pl.BlockSpec(memory_space=pltpu.SMEM)


def attend(side, state, proj, mask):
    return pl.pallas_call(
        attend_kernel,
        out_shape=jax.ShapeDtypeStruct(state.shape, BF16),
        in_specs=[SMEM, VMEM, VMEM, VMEM],
        out_specs=VMEM,
        compiler_params=pltpu.CompilerParams(vmem_limit_bytes=KERNEL_VMEM),
        name="attend",
    )(side, state, proj, mask)


def pull_kernel(side_ref, proj_ref, mask_ref, own_ref, edge_ref, out_ref):
    rows, width = own_ref.shape
    size = width // HEADS
    scale = size ** (-0.5)
    cuts = spans(width, size)
    half = rows // 2
    below = 2 - side_ref[0]
    above = 3 - below

    def low_queries(a, b):
        return rows_of(proj_ref[below, half:, a:b], proj_ref[0, :half, a:b])

    def high_queries(a, b):
        return rows_of(proj_ref[0, half:, a:b], proj_ref[above, :half, a:b])

    def low_keys(a, b):
        return rows_of(proj_ref[below, :, a:b], proj_ref[0, :, a:b])

    def high_keys(a, b):
        return rows_of(proj_ref[0, :, a:b], proj_ref[above, :, a:b])

    def both(low, high, base):
        return [low(base + a, base + b) for a, b in cuts] + [
            high(base + a, base + b) for a, b in cuts
        ]

    queries = both(low_queries, high_queries, 0)
    keys = both(low_keys, high_keys, width)
    values = both(low_keys, high_keys, 2 * width)
    upstream = [rows_of(edge_ref[below - 1, :, a:b], own_ref[:half, a:b]) for a, b in cuts] + [
        rows_of(own_ref[half:, a:b], edge_ref[above - 1, :, a:b]) for a, b in cuts
    ]
    used = [mask_ref[0] > 0] * HEADS + [mask_ref[1] > 0] * HEADS
    probs = softmax_band(queries, keys, used, scale)
    grad_probs = [nt(u, v).astype(BF16).astype(F32) for u, v in zip(upstream, values)]
    inner = [jnp.sum(g * p, axis=-1, keepdims=True) for g, p in zip(grad_probs, probs)]
    grad_scores = [
        (p * (g - i) * scale).astype(BF16) for p, g, i in zip(probs, grad_probs, inner)
    ]
    rounded = [p.astype(BF16) for p in probs]
    for head, (a, b) in enumerate(cuts):
        low, high = head, HEADS + head
        out_ref[:half, a:b] = nn(grad_scores[low], keys[low])[half:].astype(BF16)
        out_ref[half:, a:b] = nn(grad_scores[high], keys[high])[:half].astype(BF16)
        for base, left, right in ((width, grad_scores, queries), (2 * width, rounded, upstream)):
            total = tn(left[low], right[low])[rows:] + tn(left[high], right[high])[:rows]
            out_ref[:, base + a : base + b] = total.astype(BF16)


def attend_pull(side, proj, masks, own, edges):
    return pl.pallas_call(
        pull_kernel,
        out_shape=jax.ShapeDtypeStruct(proj.shape[1:], BF16),
        in_specs=[SMEM, VMEM, VMEM, VMEM, VMEM],
        out_specs=VMEM,
        compiler_params=pltpu.CompilerParams(vmem_limit_bytes=KERNEL_VMEM),
        name="attend_pull",
    )(side, proj, masks, own, edges)


def cycle(axis, steps):
    count = lax.axis_size(axis)
    return [(i, (i + steps) % count) for i in range(count)]


def place_kernel(place_ref, *refs):
    out_ref = refs[-1]
    zs, xs = 8, 4
    held = len(refs) // 2
    split = held - zs
    rows = out_ref.shape[0] // (2 * zs * xs)
    z, x, core = place_ref[0], place_ref[1], place_ref[2]
    for step in range(zs):
        for hop in range(xs):
            for side in range(2):
                index = (((z + zs - step) % zs) * xs + (x + xs - hop) % xs) * 2 + (core + side) % 2
                to = pl.multiple_of(index * rows, rows)
                piece, start = step, hop
                if step == zs // 2:
                    piece, start = step + hop // (xs // 2) * split, hop % (xs // 2)
                elif step > zs // 2:
                    piece = step + split
                source = refs[side * held + piece]
                out_ref[pl.ds(to, rows), :] = source[start * rows : (start + 1) * rows, :]


def gather_column(shard):
    hops = [shard] + [lax.ppermute(shard, "x", cycle("x", hop)) for hop in range(1, 4)]
    return jnp.concatenate(hops, axis=0)


def ring_step(ahead, back):
    return lax.ppermute(ahead, "z", cycle("z", 1)), lax.ppermute(back, "z", cycle("z", -1))


def place_weights(own):
    other = [swap(piece) for piece in own]
    place = jnp.stack([lax.axis_index(axis) for axis in NODE]).astype(jnp.int32)
    return pl.pallas_call(
        place_kernel,
        out_shape=jax.ShapeDtypeStruct(
            (2 * sum(piece.shape[0] for piece in own), own[0].shape[1]), BF16
        ),
        in_specs=[SMEM] + [VMEM] * (2 * len(own)),
        out_specs=VMEM,
        compiler_params=pltpu.CompilerParams(vmem_limit_bytes=2 * KERNEL_VMEM),
        name="place_weights",
    )(place, *own, *other)


def route_out(obs_rows, obs_device, obs_node, micro):
    per_dev, levels = obs_rows.shape[1:]
    node_devs = lax.axis_size(NODE)
    capacity = max(2, 2 * per_dev // node_devs)
    slots = node_devs * micro * capacity
    target = obs_device[..., 0]
    named = (target[..., None] == jnp.arange(node_devs)[None, None, :]).astype(BF16)
    earlier = (jnp.arange(per_dev)[:, None] > jnp.arange(per_dev)[None, :]).astype(BF16)
    before = jnp.einsum("ij,mjd->mid", earlier, named, preferred_element_type=F32)
    ranked = jnp.sum(before * named.astype(F32), axis=-1).astype(jnp.int32)
    position = (target * micro + jnp.arange(micro)[:, None]) * capacity + ranked
    chosen = (jnp.arange(slots)[:, None] == position.reshape(1, -1)).astype(BF16)
    payload = jnp.concatenate([obs_rows, obs_node[..., None].astype(BF16)], axis=-1)
    sent = nn(chosen, payload.reshape(micro * per_dev, levels + 1)).astype(BF16)
    return sent.reshape(node_devs, micro * capacity, levels + 1)


def route_in(received, encode_weight, node_state):
    micro, nodes_dev, width = node_state.shape
    node_devs, held_slots, columns = received.shape
    levels, slots, capacity = columns - 1, node_devs * held_slots, held_slots // micro
    received = received.reshape(slots, columns)
    owner = received[:, levels].astype(jnp.int32)
    owner = owner + (jnp.arange(slots) // capacity % micro) * nodes_dev
    held = (jnp.arange(micro * nodes_dev)[:, None] == owner[None, :]).astype(BF16)
    summed = nn(held, received[:, :levels])
    high = lax.reduce_precision(summed, 8, 7)
    rest = summed - high
    encoded = nn(high.astype(BF16), encode_weight) + nn(rest.astype(BF16), encode_weight)
    return (node_state.astype(F32) + encoded.reshape(micro, nodes_dev, width)).astype(BF16)


def body(
    master,
    first_moment,
    second_moment,
    node_state,
    obs_rows,
    obs_device,
    obs_node,
    encode_weight,
    decode_weight,
    neighbors,
    neighbor_count,
    out_grad,
):
    sections = lax.axis_size("section")
    section = lax.axis_index("section")
    node_devs = lax.axis_size(NODE)
    micro, nodes_dev, width = node_state.shape
    total_nodes = nodes_dev * node_devs
    anchor = lax.axis_index(NODE) * nodes_dev
    plane = lax.axis_size(PLANE)
    sent = route_out(obs_rows, obs_device, obs_node, micro)
    column = gather_column(master[0].astype(BF16))
    sent, column = lax.optimization_barrier((sent, column))
    received = lax.all_to_all(sent, NODE, split_axis=0, concat_axis=0, tiled=True)
    first = ring_step(column, column)
    second = ring_step(*first)
    received, second = lax.optimization_barrier((received, second))
    core = lax.axis_index("core")
    side = core.astype(jnp.int32).reshape(1)
    half = nodes_dev // 2

    def pair_edge(value, first):
        return jnp.where(first, value[..., half:, :], value[..., :half, :])

    def cross_edge(value, first):
        return jnp.where(first, value[..., :half, :], value[..., half:, :])

    entry = route_in(received, encode_weight, node_state)
    rim = HALO_W
    relative = (neighbors - anchor) % total_nodes
    relative = jnp.where(relative >= total_nodes - rim, relative - total_nodes, relative) + rim
    relative = relative - half * (jnp.arange(nodes_dev)[:, None] // half)
    reach = half + 2 * rim
    valid = jnp.arange(neighbors.shape[1])[None, :] < neighbor_count[:, None]
    at = (relative[..., None] == jnp.arange(reach)[None, None, :]) & valid[..., None]
    near = jnp.sum(at.astype(F32), axis=1).astype(BF16)
    head_grad = nt(out_grad.reshape(micro * nodes_dev, -1), decode_weight)
    head_grad = head_grad.astype(BF16).reshape(micro, nodes_dev, width)

    def packed(edge):
        return jnp.concatenate(
            [
                edge(head_grad, core == 0).reshape(-1, width),
                jnp.pad(edge(near, core == 0), ((0, 0), (0, width - reach))),
            ]
        )

    from_pair = swap(packed(pair_edge))
    from_cross = beside(jnp.concatenate([packed(cross_edge), entry.reshape(-1, width)]), 0)
    third = ring_step(*second)
    cut = column.shape[0] // 2
    halves = third[0][:cut], third[1][cut:]
    fourth = ring_step(*halves)
    from_cross, fourth = lax.optimization_barrier((from_cross, fourth))
    pieces = [column, first[0], second[0], third[0], *fourth, third[1], second[1], first[1]]
    x = lax.axis_index("x")
    turns = [((x + 4 - source) % 4).astype(jnp.uint32) for source in range(4)]
    at_stage = [section == stage for stage in range(sections)]
    heads = micro * half
    head_pair = [from_pair[i * half : (i + 1) * half] for i in range(micro)]
    head_cross = [from_cross[i * half : (i + 1) * half] for i in range(micro)]
    near_pair = from_pair[heads : heads + half, :reach]
    near_cross = from_cross[heads : heads + half, :reach]
    entry_cross = [
        from_cross[heads + half + i * nodes_dev : heads + half + (i + 1) * nodes_dev]
        for i in range(micro)
    ]
    near_low = jnp.where(core == 0, near_cross, near_pair)
    near_high = jnp.where(core == 0, near_pair, near_cross)

    def bands(upper, lower):
        room = 2 * nodes_dev - reach
        return jnp.concatenate(
            [jnp.pad(upper, ((0, 0), (0, room))), jnp.pad(lower, ((0, 0), (room, 0)))]
        ).astype(F32)

    ready = dict(
        mask=bands(near[:half], near[half:]),
        masks=jnp.stack([bands(near_low, near[:half]), bands(near[half:], near_high)]),
        entry=[entry[i] for i in range(micro)],
        entry_pair=swap(entry[0]),
        entry_cross=entry_cross,
        head_grad=[head_grad[i] for i in range(micro)],
        head_pair=head_pair,
        head_cross=head_cross,
        first_core=core == 0,
        side=side,
        at_stage=at_stage,
        turns=turns,
    )
    ready = lax.optimization_barrier(ready)
    mask, masks, entry, entry_cross = (
        ready[name] for name in ("mask", "masks", "entry", "entry_cross")
    )
    head_grad, head_pair, head_cross = (
        ready[name] for name in ("head_grad", "head_pair", "head_cross")
    )
    first_core, side, at_stage, turns = (
        ready[name] for name in ("first_core", "side", "at_stage", "turns")
    )
    weight_full = place_weights(pieces)

    ticks = micro + sections - 1
    incoming, incoming_cross = None, None
    saved = []
    kept_normed = [None] * micro
    for tick in range(ticks):
        state, cross = incoming, incoming_cross
        if tick == 0:
            state, cross = entry[0], entry_cross[0]
        elif tick < micro:
            state = jnp.where(at_stage[0], entry[tick], incoming)
            cross = jnp.where(at_stage[0], entry_cross[tick], incoming_cross)
        pair = ready["entry_pair"] if tick == 0 else swap(state)
        around = jnp.concatenate([state, pair, cross], axis=0)
        normed = norm_rows(around.astype(F32)).astype(BF16)
        proj = nn(normed, weight_full).astype(BF16).reshape(3, nodes_dev, 3 * width)
        saved.append((state, proj))
        for batch in range(micro):
            stage = tick - batch
            if stage == 0:
                kept_normed[batch] = normed[:nodes_dev]
            elif 0 < stage < sections:
                kept_normed[batch] = jnp.where(
                    at_stage[stage], normed[:nodes_dev], kept_normed[batch]
                )
        if tick + 1 < ticks:
            output = attend(side, state, proj, mask)
            incoming_cross = beside(output, 1)
            incoming = from_behind(output, "section", 1)
    kept = jnp.concatenate(kept_normed, axis=0)
    hops = [kept] + [lax.ppermute(kept, "x", cycle("x", hop)) for hop in range(1, 4)]
    hops = jnp.stack(hops)
    mine = jnp.stack([lax.dynamic_index_in_dim(hops, turn, 0, False) for turn in turns])
    theirs = swap(mine)
    normed_all = jnp.stack(
        [jnp.where(first_core, mine, theirs), jnp.where(first_core, theirs, mine)], axis=1
    )
    returning, returning_cross = None, None
    columns = 3 * width // plane
    kept_grad = [None] * micro
    for tick in range(ticks):
        sources = {}
        for stage in range(sections):
            batch = tick - (sections - 1) + stage
            if 0 <= batch < micro:
                sources[stage] = (batch, batch + stage)
        stages = sorted(sources)
        state, proj = saved[sources[stages[0]][1]]
        for stage in stages[1:]:
            here = at_stage[stage]
            state, proj = (
                jnp.where(here, a, b) for a, b in zip(saved[sources[stage][1]], (state, proj))
            )
        last = sections - 1
        if last not in sources:
            own, pair, cross = returning, swap(pair_edge(returning, first_core)), returning_cross
        elif tick == 0:
            own, pair, cross = head_grad[0], head_pair[0], head_cross[0]
        else:
            batch = sources[last][0]
            own = jnp.where(at_stage[last], head_grad[batch], returning)
            cross = jnp.where(at_stage[last], head_cross[batch], returning_cross)
            pair = swap(pair_edge(own, first_core))
        grad_qkv = attend_pull(side, proj, masks, own, jnp.stack([pair, cross]))
        for stage in stages:
            batch = sources[stage][0]
            if kept_grad[batch] is None:
                kept_grad[batch] = grad_qkv
            else:
                kept_grad[batch] = jnp.where(at_stage[stage], grad_qkv, kept_grad[batch])
        if tick + 1 < ticks:
            grad_normed = nt(grad_qkv, weight_full)
            downward = (own.astype(F32) + norm_pull(state.astype(F32), grad_normed)).astype(BF16)
            returning_cross = beside(cross_edge(downward, first_core), -1)
            returning = from_behind(downward, "section", -1)
    parts = jnp.concatenate(kept_grad, axis=0).reshape(micro * nodes_dev, plane, columns)
    gathered = lax.all_to_all(
        parts.transpose(1, 0, 2), PLANE, split_axis=0, concat_axis=0, tiled=True
    )
    partial = tn(
        normed_all.reshape(plane * micro * nodes_dev, width),
        gathered.reshape(plane * micro * nodes_dev, columns),
    )
    rows = width // node_devs
    pieces = lax.all_to_all(
        partial.astype(BF16).reshape(node_devs, rows, columns),
        NODE,
        split_axis=0,
        concat_axis=0,
        tiled=True,
    )
    pieces = pieces.reshape(node_devs // plane, plane, rows, columns).astype(F32)
    gradient = jnp.sum(pieces, axis=0).transpose(1, 0, 2).reshape(1, rows, 3 * width)
    new_first = BETA_ONE * first_moment + (1.0 - BETA_ONE) * gradient
    new_second = BETA_TWO * second_moment + (1.0 - BETA_TWO) * gradient * gradient
    step_size = (
        new_first / (1.0 - BETA_ONE**STEP) / (jnp.sqrt(new_second / (1.0 - BETA_TWO**STEP)) + 1e-08)
    )
    new_weights = master - LEARN_RATE * step_size
    return (new_weights, new_first, new_second)


def solution(mesh):
    sections, node_devs = mesh.devices.shape
    fine = Mesh(mesh.devices.reshape(sections, node_devs // 8, 4, 2), ("section",) + NODE)
    in_specs = (
        P("section", NODE, None),
        P("section", NODE, None),
        P("section", NODE, None),
        P(None, NODE, None),
        P(None, NODE, None),
        P(None, NODE, None),
        P(None, NODE),
        P(),
        P(),
        P(NODE, None),
        P(NODE),
        P(None, NODE, None),
    )
    out_specs = (P("section", NODE, None), P("section", NODE, None), P("section", NODE, None))
    return jax.shard_map(body, mesh=fine, in_specs=in_specs, out_specs=out_specs, check_vma=False)
```

```python
import jax
import jax.numpy as jnp
from jax import lax
from jax.experimental import pallas as pl
from jax.experimental.pallas import tpu as pltpu
from jax.sharding import Mesh, PartitionSpec as P

HEADS = 8
HALO_W = 32
STEP = 100


BETA_ONE = 0.9
BETA_TWO = 0.999
LEARN_RATE = 0.001

NODE = ("z", "x", "core")
PLANE = ("x", "core")
F32 = jnp.float32
BF16 = jnp.bfloat16
KERNEL_VMEM = 12 * 2**20


def across(index, count):
    return (index + 1) % count if index % 2 else (index - 1) % count


def swap(value):
    return lax.ppermute(value, "core", [(0, 1), (1, 0)])


def beside(value, steps):
    sections, count = lax.axis_size("section"), lax.axis_size(NODE)
    moves = [
        (section * count + index, (section + steps) * count + across(index, count))
        for section in range(sections)
        if 0 <= section + steps < sections
        for index in range(count)
    ]
    return lax.ppermute(value, ("section",) + NODE, moves)


def from_behind(value, axis, steps):
    count = lax.axis_size(axis)
    leading, last = (max(0, -steps), min(count, count - steps))
    return lax.ppermute(value, axis, [(source, source + steps) for source in range(leading, last)])


def norm_rows(values):
    return values * lax.rsqrt(jnp.mean(values * values, axis=-1, keepdims=True) + 1e-06)


def norm_pull(values, grads):
    scale = lax.rsqrt(jnp.mean(values * values, axis=-1, keepdims=True) + 1e-06)
    inner = jnp.mean(values * grads, axis=-1, keepdims=True)
    return scale * (grads - values * (inner * scale * scale))


def nt(a, b):
    return lax.dot_general(a, b, (((1,), (1,)), ((), ())), preferred_element_type=F32)


def nn(a, b):
    return lax.dot_general(a, b, (((1,), (0,)), ((), ())), preferred_element_type=F32)


def tn(a, b):
    return lax.dot_general(a, b, (((0,), (0,)), ((), ())), preferred_element_type=F32)


def spans(width, size):
    return [(start, start + size) for start in range(0, width, size)]


def rows_of(*pieces):
    return jnp.concatenate(pieces, axis=0)


def softmax_band(queries, keys, used, scale):
    scores = [nt(query, key) * scale for query, key in zip(queries, keys)]
    weights = [jnp.where(u, jnp.exp(score), 0.0) for u, score in zip(used, scores)]
    sums = [jnp.sum(weight, axis=-1, keepdims=True) for weight in weights]
    return [weight / total for weight, total in zip(weights, sums)]


def attend_kernel(side_ref, state_ref, proj_ref, mask_ref, out_ref):
    rows, width = state_ref.shape
    size = width // HEADS
    cuts = spans(width, size)
    half = rows // 2
    below = 2 - side_ref[0]
    above = 3 - below
    used = [mask_ref[...] > 0] * HEADS

    def banded(base):
        return [
            rows_of(
                proj_ref[below, half:, base + a : base + b],
                proj_ref[0, :, base + a : base + b],
                proj_ref[above, :half, base + a : base + b],
            )
            for a, b in cuts
        ]

    queries = [proj_ref[0, :, a:b] for a, b in cuts]
    probs = softmax_band(queries, banded(width), used, size ** (-0.5))
    mixed = [nn(p.astype(BF16), v) for p, v in zip(probs, banded(2 * width))]
    for (a, b), term in zip(cuts, mixed):
        out_ref[:, a:b] = (state_ref[:, a:b].astype(F32) + term).astype(BF16)


VMEM = pl.BlockSpec(memory_space=pltpu.VMEM)
SMEM = pl.BlockSpec(memory_space=pltpu.SMEM)


def attend(side, state, proj, mask):
    return pl.pallas_call(
        attend_kernel,
        out_shape=jax.ShapeDtypeStruct(state.shape, BF16),
        in_specs=[SMEM, VMEM, VMEM, VMEM],
        out_specs=VMEM,
        compiler_params=pltpu.CompilerParams(vmem_limit_bytes=KERNEL_VMEM),
        name="attend",
    )(side, state, proj, mask)


def pull_kernel(side_ref, proj_ref, mask_ref, own_ref, edge_ref, out_ref):
    rows, width = own_ref.shape
    size = width // HEADS
    scale = size ** (-0.5)
    cuts = spans(width, size)
    half = rows // 2
    below = 2 - side_ref[0]
    above = 3 - below

    def low_queries(a, b):
        return rows_of(proj_ref[below, half:, a:b], proj_ref[0, :half, a:b])

    def high_queries(a, b):
        return rows_of(proj_ref[0, half:, a:b], proj_ref[above, :half, a:b])

    def low_keys(a, b):
        return rows_of(proj_ref[below, :, a:b], proj_ref[0, :, a:b])

    def high_keys(a, b):
        return rows_of(proj_ref[0, :, a:b], proj_ref[above, :, a:b])

    def both(low, high, base):
        return [low(base + a, base + b) for a, b in cuts] + [
            high(base + a, base + b) for a, b in cuts
        ]

    queries = both(low_queries, high_queries, 0)
    keys = both(low_keys, high_keys, width)
    values = both(low_keys, high_keys, 2 * width)
    upstream = [rows_of(edge_ref[below - 1, :, a:b], own_ref[:half, a:b]) for a, b in cuts] + [
        rows_of(own_ref[half:, a:b], edge_ref[above - 1, :, a:b]) for a, b in cuts
    ]
    used = [mask_ref[0] > 0] * HEADS + [mask_ref[1] > 0] * HEADS
    probs = softmax_band(queries, keys, used, scale)
    grad_probs = [nt(u, v).astype(BF16).astype(F32) for u, v in zip(upstream, values)]
    inner = [jnp.sum(g * p, axis=-1, keepdims=True) for g, p in zip(grad_probs, probs)]
    grad_scores = [
        (p * (g - i) * scale).astype(BF16) for p, g, i in zip(probs, grad_probs, inner)
    ]
    rounded = [p.astype(BF16) for p in probs]
    for head, (a, b) in enumerate(cuts):
        low, high = head, HEADS + head
        out_ref[:half, a:b] = nn(grad_scores[low], keys[low])[half:].astype(BF16)
        out_ref[half:, a:b] = nn(grad_scores[high], keys[high])[:half].astype(BF16)
        for base, left, right in ((width, grad_scores, queries), (2 * width, rounded, upstream)):
            total = tn(left[low], right[low])[rows:] + tn(left[high], right[high])[:rows]
            out_ref[:, base + a : base + b] = total.astype(BF16)


def attend_pull(side, proj, masks, own, edges):
    return pl.pallas_call(
        pull_kernel,
        out_shape=jax.ShapeDtypeStruct(proj.shape[1:], BF16),
        in_specs=[SMEM, VMEM, VMEM, VMEM, VMEM],
        out_specs=VMEM,
        compiler_params=pltpu.CompilerParams(vmem_limit_bytes=KERNEL_VMEM),
        name="attend_pull",
    )(side, proj, masks, own, edges)


def cycle(axis, steps):
    count = lax.axis_size(axis)
    return [(i, (i + steps) % count) for i in range(count)]


def place_kernel(place_ref, *refs):
    out_ref = refs[-1]
    zs, xs = 8, 4
    held = len(refs) // 2
    split = held - zs
    rows = out_ref.shape[0] // (2 * zs * xs)
    z, x, core = place_ref[0], place_ref[1], place_ref[2]
    for step in range(zs):
        for hop in range(xs):
            for side in range(2):
                index = (((z + zs - step) % zs) * xs + (x + xs - hop) % xs) * 2 + (core + side) % 2
                to = pl.multiple_of(index * rows, rows)
                piece, start = step, hop
                if step == zs // 2:
                    piece, start = step + hop // (xs // 2) * split, hop % (xs // 2)
                elif step > zs // 2:
                    piece = step + split
                source = refs[side * held + piece]
                out_ref[pl.ds(to, rows), :] = source[start * rows : (start + 1) * rows, :]


def gather_column(shard):
    hops = [shard] + [lax.ppermute(shard, "x", cycle("x", hop)) for hop in range(1, 4)]
    return jnp.concatenate(hops, axis=0)


def ring_step(ahead, back):
    return lax.ppermute(ahead, "z", cycle("z", 1)), lax.ppermute(back, "z", cycle("z", -1))


def place_weights(own):
    other = [swap(piece) for piece in own]
    place = jnp.stack([lax.axis_index(axis) for axis in NODE]).astype(jnp.int32)
    return pl.pallas_call(
        place_kernel,
        out_shape=jax.ShapeDtypeStruct(
            (2 * sum(piece.shape[0] for piece in own), own[0].shape[1]), BF16
        ),
        in_specs=[SMEM] + [VMEM] * (2 * len(own)),
        out_specs=VMEM,
        compiler_params=pltpu.CompilerParams(vmem_limit_bytes=2 * KERNEL_VMEM),
        name="place_weights",
    )(place, *own, *other)


def route_out(obs_rows, obs_device, obs_node, micro):
    per_dev, levels = obs_rows.shape[1:]
    node_devs = lax.axis_size(NODE)
    capacity = max(2, 2 * per_dev // node_devs)
    slots = node_devs * micro * capacity
    target = obs_device[..., 0]
    named = (target[..., None] == jnp.arange(node_devs)[None, None, :]).astype(BF16)
    earlier = (jnp.arange(per_dev)[:, None] > jnp.arange(per_dev)[None, :]).astype(BF16)
    before = jnp.einsum("ij,mjd->mid", earlier, named, preferred_element_type=F32)
    ranked = jnp.sum(before * named.astype(F32), axis=-1).astype(jnp.int32)
    position = (target * micro + jnp.arange(micro)[:, None]) * capacity + ranked
    chosen = (jnp.arange(slots)[:, None] == position.reshape(1, -1)).astype(BF16)
    payload = jnp.concatenate([obs_rows, obs_node[..., None].astype(BF16)], axis=-1)
    sent = nn(chosen, payload.reshape(micro * per_dev, levels + 1)).astype(BF16)
    return sent.reshape(node_devs, micro * capacity, levels + 1)


def route_in(received, encode_weight, node_state):
    micro, nodes_dev, width = node_state.shape
    node_devs, held_slots, columns = received.shape
    levels, slots, capacity = columns - 1, node_devs * held_slots, held_slots // micro
    received = received.reshape(slots, columns)
    owner = received[:, levels].astype(jnp.int32)
    owner = owner + (jnp.arange(slots) // capacity % micro) * nodes_dev
    held = (jnp.arange(micro * nodes_dev)[:, None] == owner[None, :]).astype(BF16)
    summed = nn(held, received[:, :levels])
    high = lax.reduce_precision(summed, 8, 7)
    rest = summed - high
    encoded = nn(high.astype(BF16), encode_weight) + nn(rest.astype(BF16), encode_weight)
    return (node_state.astype(F32) + encoded.reshape(micro, nodes_dev, width)).astype(BF16)


def body(
    master,
    first_moment,
    second_moment,
    node_state,
    obs_rows,
    obs_device,
    obs_node,
    encode_weight,
    decode_weight,
    neighbors,
    neighbor_count,
    out_grad,
):
    sections = lax.axis_size("section")
    section = lax.axis_index("section")
    node_devs = lax.axis_size(NODE)
    micro, nodes_dev, width = node_state.shape
    total_nodes = nodes_dev * node_devs
    anchor = lax.axis_index(NODE) * nodes_dev
    plane = lax.axis_size(PLANE)
    sent = route_out(obs_rows, obs_device, obs_node, micro)
    column = gather_column(master[0].astype(BF16))
    sent, column = lax.optimization_barrier((sent, column))
    received = lax.all_to_all(sent, NODE, split_axis=0, concat_axis=0, tiled=True)
    first = ring_step(column, column)
    second = ring_step(*first)
    received, second = lax.optimization_barrier((received, second))
    core = lax.axis_index("core")
    side = core.astype(jnp.int32).reshape(1)
    half = nodes_dev // 2

    def pair_edge(value, first):
        return jnp.where(first, value[..., half:, :], value[..., :half, :])

    def cross_edge(value, first):
        return jnp.where(first, value[..., :half, :], value[..., half:, :])

    entry = route_in(received, encode_weight, node_state)
    rim = HALO_W
    relative = (neighbors - anchor) % total_nodes
    relative = jnp.where(relative >= total_nodes - rim, relative - total_nodes, relative) + rim
    relative = relative - half * (jnp.arange(nodes_dev)[:, None] // half)
    reach = half + 2 * rim
    valid = jnp.arange(neighbors.shape[1])[None, :] < neighbor_count[:, None]
    at = (relative[..., None] == jnp.arange(reach)[None, None, :]) & valid[..., None]
    near = jnp.sum(at.astype(F32), axis=1).astype(BF16)
    head_grad = nt(out_grad.reshape(micro * nodes_dev, -1), decode_weight)
    head_grad = head_grad.astype(BF16).reshape(micro, nodes_dev, width)

    def packed(edge):
        return jnp.concatenate(
            [
                edge(head_grad, core == 0).reshape(-1, width),
                jnp.pad(edge(near, core == 0), ((0, 0), (0, width - reach))),
            ]
        )

    from_pair = swap(packed(pair_edge))
    from_cross = beside(jnp.concatenate([packed(cross_edge), entry.reshape(-1, width)]), 0)
    third = ring_step(*second)
    cut = column.shape[0] // 2
    halves = third[0][:cut], third[1][cut:]
    fourth = ring_step(*halves)
    from_cross, fourth = lax.optimization_barrier((from_cross, fourth))
    pieces = [column, first[0], second[0], third[0], *fourth, third[1], second[1], first[1]]
    x = lax.axis_index("x")
    turns = [((x + 4 - source) % 4).astype(jnp.uint32) for source in range(4)]
    at_stage = [section == stage for stage in range(sections)]
    heads = micro * half
    head_pair = [from_pair[i * half : (i + 1) * half] for i in range(micro)]
    head_cross = [from_cross[i * half : (i + 1) * half] for i in range(micro)]
    near_pair = from_pair[heads : heads + half, :reach]
    near_cross = from_cross[heads : heads + half, :reach]
    entry_cross = [
        from_cross[heads + half + i * nodes_dev : heads + half + (i + 1) * nodes_dev]
        for i in range(micro)
    ]
    near_low = jnp.where(core == 0, near_cross, near_pair)
    near_high = jnp.where(core == 0, near_pair, near_cross)

    def bands(upper, lower):
        room = 2 * nodes_dev - reach
        return jnp.concatenate(
            [jnp.pad(upper, ((0, 0), (0, room))), jnp.pad(lower, ((0, 0), (room, 0)))]
        ).astype(F32)

    ready = dict(
        mask=bands(near[:half], near[half:]),
        masks=jnp.stack([bands(near_low, near[:half]), bands(near[half:], near_high)]),
        entry=[entry[i] for i in range(micro)],
        entry_pair=swap(entry[0]),
        entry_cross=entry_cross,
        head_grad=[head_grad[i] for i in range(micro)],
        head_pair=head_pair,
        head_cross=head_cross,
        first_core=core == 0,
        side=side,
        at_stage=at_stage,
        turns=turns,
    )
    ready = lax.optimization_barrier(ready)
    mask, masks, entry, entry_cross = (
        ready[name] for name in ("mask", "masks", "entry", "entry_cross")
    )
    head_grad, head_pair, head_cross = (
        ready[name] for name in ("head_grad", "head_pair", "head_cross")
    )
    first_core, side, at_stage, turns = (
        ready[name] for name in ("first_core", "side", "at_stage", "turns")
    )
    weight_full = place_weights(pieces)

    ticks = micro + sections - 1
    incoming, incoming_cross = None, None
    saved = []
    kept_normed = [None] * micro
    for tick in range(ticks):
        state, cross = incoming, incoming_cross
        if tick == 0:
            state, cross = entry[0], entry_cross[0]
        elif tick < micro:
            state = jnp.where(at_stage[0], entry[tick], incoming)
            cross = jnp.where(at_stage[0], entry_cross[tick], incoming_cross)
        pair = ready["entry_pair"] if tick == 0 else swap(state)
        around = jnp.concatenate([state, pair, cross], axis=0)
        normed = norm_rows(around.astype(F32)).astype(BF16)
        proj = nn(normed, weight_full).astype(BF16).reshape(3, nodes_dev, 3 * width)
        saved.append((state, proj))
        for batch in range(micro):
            stage = tick - batch
            if stage == 0:
                kept_normed[batch] = normed[:nodes_dev]
            elif 0 < stage < sections:
                kept_normed[batch] = jnp.where(
                    at_stage[stage], normed[:nodes_dev], kept_normed[batch]
                )
        if tick + 1 < ticks:
            output = attend(side, state, proj, mask)
            if tick == sections - 1:
                early_grad = attend_pull(
                    side, proj, masks, head_grad[0], jnp.stack([head_pair[0], head_cross[0]])
                )
                early_down = head_grad[0].astype(F32) + norm_pull(
                    state.astype(F32), nt(early_grad, weight_full)
                )
                output, early_grad, early_down = lax.optimization_barrier(
                    (output, early_grad, early_down.astype(BF16))
                )
            incoming_cross = beside(output, 1)
            incoming = from_behind(output, "section", 1)
    kept = jnp.concatenate(kept_normed, axis=0)
    hops = [kept] + [lax.ppermute(kept, "x", cycle("x", hop)) for hop in range(1, 4)]
    hops = jnp.stack(hops)
    mine = jnp.stack([lax.dynamic_index_in_dim(hops, turn, 0, False) for turn in turns])
    theirs = swap(mine)
    normed_all = jnp.stack(
        [jnp.where(first_core, mine, theirs), jnp.where(first_core, theirs, mine)], axis=1
    )
    returning, returning_cross = None, None
    columns = 3 * width // plane
    kept_grad = [None] * micro
    for tick in range(ticks):
        sources = {}
        for stage in range(sections):
            batch = tick - (sections - 1) + stage
            if 0 <= batch < micro:
                sources[stage] = (batch, batch + stage)
        stages = sorted(sources)
        state, proj = saved[sources[stages[0]][1]]
        for stage in stages[1:]:
            here = at_stage[stage]
            state, proj = (
                jnp.where(here, a, b) for a, b in zip(saved[sources[stage][1]], (state, proj))
            )
        last = sections - 1
        if last not in sources:
            own, pair, cross = returning, swap(pair_edge(returning, first_core)), returning_cross
        elif tick == 0:
            own, pair, cross = head_grad[0], head_pair[0], head_cross[0]
        else:
            batch = sources[last][0]
            own = jnp.where(at_stage[last], head_grad[batch], returning)
            cross = jnp.where(at_stage[last], head_cross[batch], returning_cross)
            pair = swap(pair_edge(own, first_core))
        if tick == 0:
            grad_qkv = early_grad
        else:
            grad_qkv = attend_pull(side, proj, masks, own, jnp.stack([pair, cross]))
        for stage in stages:
            batch = sources[stage][0]
            if kept_grad[batch] is None:
                kept_grad[batch] = grad_qkv
            else:
                kept_grad[batch] = jnp.where(at_stage[stage], grad_qkv, kept_grad[batch])
        if tick + 1 < ticks:
            if tick == 0:
                downward = early_down
            else:
                grad_normed = nt(grad_qkv, weight_full)
                downward = own.astype(F32) + norm_pull(state.astype(F32), grad_normed)
                downward = downward.astype(BF16)
            returning_cross = beside(cross_edge(downward, first_core), -1)
            returning = from_behind(downward, "section", -1)
    parts = jnp.concatenate(kept_grad, axis=0).reshape(micro * nodes_dev, plane, columns)
    gathered = lax.all_to_all(
        parts.transpose(1, 0, 2), PLANE, split_axis=0, concat_axis=0, tiled=True
    )
    partial = tn(
        normed_all.reshape(plane * micro * nodes_dev, width),
        gathered.reshape(plane * micro * nodes_dev, columns),
    )
    rows = width // node_devs
    pieces = lax.all_to_all(
        partial.astype(BF16).reshape(node_devs, rows, columns),
        NODE,
        split_axis=0,
        concat_axis=0,
        tiled=True,
    )
    pieces = pieces.reshape(node_devs // plane, plane, rows, columns).astype(F32)
    gradient = jnp.sum(pieces, axis=0).transpose(1, 0, 2).reshape(1, rows, 3 * width)
    new_first = BETA_ONE * first_moment + (1.0 - BETA_ONE) * gradient
    new_second = BETA_TWO * second_moment + (1.0 - BETA_TWO) * gradient * gradient
    step_size = (
        new_first / (1.0 - BETA_ONE**STEP) / (jnp.sqrt(new_second / (1.0 - BETA_TWO**STEP)) + 1e-08)
    )
    new_weights = master - LEARN_RATE * step_size
    return (new_weights, new_first, new_second)


def solution(mesh):
    sections, node_devs = mesh.devices.shape
    fine = Mesh(mesh.devices.reshape(sections, node_devs // 8, 4, 2), ("section",) + NODE)
    in_specs = (
        P("section", NODE, None),
        P("section", NODE, None),
        P("section", NODE, None),
        P(None, NODE, None),
        P(None, NODE, None),
        P(None, NODE, None),
        P(None, NODE),
        P(),
        P(),
        P(NODE, None),
        P(NODE),
        P(None, NODE, None),
    )
    out_specs = (P("section", NODE, None), P("section", NODE, None), P("section", NODE, None))
    return jax.shard_map(body, mesh=fine, in_specs=in_specs, out_specs=out_specs, check_vma=False)
```
